256 devices in a mesh: sub: 64 (over x, z, core), grp: 4 (over y).
Axes of the slice: x: 4, y: 4, z: 8, core: 2. Of those that a mesh axis runs over, the one named last changes fastest.
Arguments:
- multipliers: float32 [64, 4, 64, 1200], P('sub', 'grp'), as said below
- residual: float32 [64, 4, 64, 1200], P('sub', 'grp'), as said below
- direction: float32 [64, 4, 64, 1200], P('sub', 'grp'), as said below
- dual_operator: float32 [64, 4, 1200, 1200], P('sub', 'grp'), as said below
- rigid_trace: float32 [64, 4, 6, 1200], P('sub', 'grp'), may hold values from -0.375 to 0.375
- coarse_inverse: float32 [1536, 1536], P(('sub', 'grp'))
- face_sizes: int32 [64, 4, 4], P('sub', 'grp'), may hold values from 0 to 300, as said below
- slot_order: int32 [64, 4, 1200], P('sub', 'grp'), may hold values from 0 to 1199, each once within a row
Outputs:
- multipliers_next: float32 [64, 4, 64, 1200], P('sub', 'grp')
- residual_next: float32 [64, 4, 64, 1200], P('sub', 'grp')
- direction_next: float32 [64, 4, 64, 1200], P('sub', 'grp')
The draws below stay inside these ranges and needn't reach their ends.
Inputs may be any that keep to these rules, and one draw needn't show every extreme that they name: `face_sizes`: face 0 of every subdomain with s = 0, face 1 with s = 63, face 2 with g = 0 and face 3 with g = 3 have size 0; the two faces that two subdomains share have equal sizes; the size 300 occurs in every draw. `multipliers`: where two subdomains share a face, their copies agree place by place: face 1 of (s, g) equals face 0 of (s + 1, g), face 3 of (s, g) equals face 2 of (s, g + 1). `residual`: copies on shared faces agree as for multipliers. `direction`: copies on shared faces agree as for multipliers. `dual_operator`: each block has a positive definite symmetric part.
All inputs are finite; a program needn't handle non-finite values.
Results may differ from the reference program's by a relative error of at most 0.000062.
Values sent between devices are 32-bit elements; how exact they have to be, the bound alone decides.
A program may use at most 64 MiB of HBM per device.

```python
import math
import jax
import jax.numpy as jnp
from jax import lax

FW = 300
M = 1200
MODES = 6
CASES = 64
SUBS = 64
GROUPS = 4
COARSE = 1536


def face_copies(edges):
    along_sub = edges[:, :, :, 0]
    along_grp = edges[:, :, :, 1]
    zero_sub = jnp.zeros_like(along_sub[:1])
    zero_grp = jnp.zeros_like(along_grp[:, :1])
    face_zero = jnp.concatenate([zero_sub, along_sub[:-1]], axis=0)
    face_two = jnp.concatenate([zero_grp, along_grp[:, :-1]], axis=1)
    stacked = jnp.stack([face_zero, along_sub, face_two, along_grp], axis=3)
    return stacked.reshape(SUBS, GROUPS, CASES, M)


def shaped_edges(base, key):
    spread = jnp.exp(jax.random.uniform(key, (SUBS, GROUPS, 1, 2, FW), jnp.float32) * math.log(10.0))
    rise = 1.0 + 2.0 * jnp.arange(SUBS, dtype=jnp.float32) / max(SUBS - 1, 1)
    return face_copies(base * spread * rise[:, None, None, None, None])


def draw_multipliers(key, part):
    key = jax.random.fold_in(key, 11)
    first, second = jax.random.split(key)
    shape = (SUBS, GROUPS, CASES, 2, FW)
    base = jax.random.normal(first, shape, jnp.float32)
    return shaped_edges(base, second)


def draw_residual(key, part):
    key = jax.random.fold_in(key, 12)
    first, second = jax.random.split(key)
    shape = (SUBS, GROUPS, CASES, 2, FW)
    base = jax.random.normal(first, shape, jnp.float32)
    return shaped_edges(base, second)


def draw_direction(key, part):
    key = jax.random.fold_in(key, 13)
    first, second = jax.random.split(key)
    shape = (SUBS, GROUPS, CASES, 2, FW)
    base = jax.random.normal(first, shape, jnp.float32)
    return shaped_edges(base, second)


def draw_dual_operator(key, part):
    key = jax.random.fold_in(key, 14)
    first, second = jax.random.split(key)
    shape = (SUBS, GROUPS, M, M)
    noise = jax.random.normal(first, shape, jnp.float32)
    diagonal = jax.random.uniform(second, (SUBS, GROUPS, M), jnp.float32, 1.5, 3.0)
    index = jnp.arange(M, dtype=jnp.int32)
    eye = (index[:, None] == index[None, :]).astype(jnp.float32)
    return noise * (0.7 / math.sqrt(M)) + eye * diagonal[:, :, :, None]


def draw_coarse_inverse(key, part):
    key = jax.random.fold_in(key, 15)
    first, second = jax.random.split(key)
    noise = jax.random.normal(first, (COARSE, COARSE), jnp.float32)
    diagonal = jax.random.uniform(second, (COARSE,), jnp.float32, 1.0, 2.0)
    index = jnp.arange(COARSE, dtype=jnp.int32)
    eye = (index[:, None] == index[None, :]).astype(jnp.float32)
    return noise * (0.5 / math.sqrt(COARSE)) + eye * diagonal[:, None]


def draw_face_sizes(key, part):
    key = jax.random.fold_in(key, 16)
    first, second = jax.random.split(key)
    rows = jnp.arange(SUBS, dtype=jnp.int32)[:, None]
    cols = jnp.arange(GROUPS, dtype=jnp.int32)[None, :]
    corner = (rows == 0) & (cols == 0)
    edge_sub = jax.random.randint(first, (SUBS, GROUPS), FW // 2, FW + 1)
    edge_sub = jnp.where(corner, FW, edge_sub)
    edge_sub = jnp.where(rows == SUBS - 1, 0, edge_sub)
    edge_grp = jax.random.randint(second, (SUBS, GROUPS), FW // 2, FW + 1)
    edge_grp = jnp.where(cols == GROUPS - 1, 0, edge_grp)
    face_zero = jnp.concatenate([jnp.zeros_like(edge_sub[:1]), edge_sub[:-1]], axis=0)
    face_two = jnp.concatenate([jnp.zeros_like(edge_grp[:, :1]), edge_grp[:, :-1]], axis=1)
    return jnp.stack([face_zero, edge_sub, face_two, edge_grp], axis=2).astype(jnp.int32)


def steps_of(own_key, dims, cuts, smallest, high):
    loudness, own = 1.0, jax.random.fold_in(own_key, 6)
    for dim, blocks in cuts:
        heights = jnp.exp(jax.random.uniform(jax.random.fold_in(own, dim), (blocks,), jnp.float32, smallest / len(cuts), high / len(cuts)))
        loudness = loudness * jnp.repeat(heights, dims[dim] // blocks).reshape([-1 if axis == dim else 1 for axis in range(len(dims))])
    return loudness


def bell_draw(key, shape, scale, reach, pieces=(), kind=jnp.bfloat16):
    result = scale * jax.random.normal(key, shape, jnp.float32)
    if pieces:
        result = result * steps_of(key, shape, pieces, -0.22, 0.18)
    return jnp.clip(result, -reach, reach).astype(kind)


def setup_inputs(seed: int = 0) -> dict:
    key_list = jax.random.split(jax.random.key(seed), 9)
    multipliers = draw_multipliers(jax.random.fold_in(key_list[8], 71), 0)
    residual = draw_residual(jax.random.fold_in(key_list[8], 71), 0)
    direction = draw_direction(jax.random.fold_in(key_list[8], 71), 0)
    dual_operator = draw_dual_operator(jax.random.fold_in(key_list[8], 71), 0)
    rigid_trace = bell_draw(key_list[4], (SUBS, GROUPS, MODES, M), (M // 4) ** -0.5, 0.375, ((0, 64), (1, 4)), jnp.float32)
    coarse_inverse = draw_coarse_inverse(jax.random.fold_in(key_list[8], 71), 0)
    face_sizes = draw_face_sizes(jax.random.fold_in(key_list[8], 71), 0)
    slot_order = jax.vmap(lambda own: jax.random.permutation(own, M))(jax.random.split(key_list[7], SUBS * GROUPS)).reshape((SUBS, GROUPS, M)).astype(jnp.int32)
    return dict(multipliers=multipliers, residual=residual, direction=direction, dual_operator=dual_operator, rigid_trace=rigid_trace, coarse_inverse=coarse_inverse, face_sizes=face_sizes, slot_order=slot_order)


def assemble(field):
    faces = field.reshape(field.shape[0], field.shape[1], field.shape[2], 4, FW)
    zero_sub = jnp.zeros_like(faces[:1, :, :, 0])
    low_sub = jnp.concatenate([zero_sub, faces[:-1, :, :, 1]], axis=0)
    high_sub = jnp.concatenate([faces[1:, :, :, 0], zero_sub], axis=0)
    zero_grp = jnp.zeros_like(faces[:, :1, :, 0])
    low_grp = jnp.concatenate([zero_grp, faces[:, :-1, :, 3]], axis=1)
    high_grp = jnp.concatenate([faces[:, 1:, :, 2], zero_grp], axis=1)
    extra = jnp.stack([low_sub, high_sub, low_grp, high_grp], axis=3).reshape(field.shape)
    return field + extra


def reference(multipliers, residual, direction, dual_operator, rigid_trace, coarse_inverse, face_sizes, slot_order):
    position = jnp.arange(M, dtype=jnp.int32)
    face_of = position // FW
    pick = face_of[None, None, None, :] == jnp.arange(4, dtype=jnp.int32)[None, None, :, None]
    limit = jnp.sum(jnp.where(pick, face_sizes[:, :, :, None], 0), axis=2)
    active = ((position % FW)[None, None, :] < limit).astype(jnp.float32)[:, :, None, :]
    face_sign = jnp.where(face_of % 2 == 0, -1.0, 1.0).astype(jnp.float32)
    slot_sign = face_sign[slot_order][:, :, None, :]
    inverse = jnp.argsort(slot_order, axis=-1).astype(jnp.int32)
    shape = multipliers.shape
    order_full = jnp.broadcast_to(slot_order[:, :, None, :], shape)
    inverse_full = jnp.broadcast_to(inverse[:, :, None, :], shape)

    def to_slots(field):
        return jnp.take_along_axis(field, order_full, axis=3) * slot_sign

    def to_faces(values):
        return jnp.take_along_axis(values * slot_sign, inverse_full, axis=3) * active

    high = lax.Precision.HIGHEST
    lam = multipliers * active
    res = residual * active
    dirn = direction * active
    applied = jnp.einsum("sgkl,sgnl->sgnk", dual_operator, to_slots(dirn), precision=high)
    image = assemble(to_faces(applied))
    rr = 0.5 * jnp.sum(res * res, axis=(0, 1, 3))
    curvature = 0.5 * jnp.sum(dirn * image, axis=(0, 1, 3))
    coarse_load = jnp.einsum("sgik,sgnk->sgin", rigid_trace, to_slots(image), precision=high)
    coarse_load = coarse_load.reshape(COARSE, shape[2])
    amplitude = jnp.dot(coarse_inverse, coarse_load, precision=high).reshape(shape[0], shape[1], MODES, shape[2])
    back = jnp.einsum("sgin,sgik->sgnk", amplitude, rigid_trace, precision=high)
    projected = image - assemble(to_faces(back))
    step = (rr / curvature)[None, None, :, None]
    multipliers_next = lam + step * dirn
    residual_next = res - step * projected
    rr_next = 0.5 * jnp.sum(residual_next * residual_next, axis=(0, 1, 3))
    direction_next = residual_next + (rr_next / rr)[None, None, :, None] * dirn
    return multipliers_next, residual_next, direction_next
```

```python
import functools

import jax
import jax.numpy as jnp
from jax import lax
from jax.experimental import pallas as pl
from jax.experimental.pallas import tpu as pltpu
from jax.sharding import PartitionSpec as P

MESH = pl.DeviceIdType.MESH
F32 = jnp.float32
BF16 = jnp.bfloat16
NN = (((1,), (0,)), ((), ()))
NT = (((1,), (1,)), ((), ()))
TN = (((0,), (0,)), ((), ()))

CASES = 64
WIDTH = 1200
FACE = 300
PAD = 384
WIDE = 4 * PAD
MODES = 6
COARSE = 1536
WINDOW = 256
MEMBERS = 16


def split(x):
    high = x.astype(BF16)
    return high, (x - high.astype(F32)).astype(BF16)


def mm(a, b, dims):
    return lax.dot_general(a, b, dims, preferred_element_type=F32)


def iota(shape, dim):
    return lax.broadcasted_iota(jnp.int32, shape, dim)


def face_at(lane, step):
    one = jnp.int32(1)
    zero = jnp.int32(0)
    return (
        jnp.where(lane >= step, one, zero)
        + jnp.where(lane >= 2 * step, one, zero)
        + jnp.where(lane >= 3 * step, one, zero)
    )


def row_of(column):
    eye = iota((CASES, 128), 0) == iota((CASES, 128), 1)
    return jnp.sum(jnp.where(eye, column, 0.0), axis=0, keepdims=True)


def column_of(row):
    eye = iota((CASES, 128), 0) == iota((CASES, 128), 1)
    return jnp.sum(jnp.where(eye, row, 0.0), axis=1, keepdims=True)


def window_start(block):
    return min(max(((96 * block - 24) // 128) * 128, 0), COARSE - WINDOW)


def kernel(
    lam_hbm,
    res_hbm,
    dir_hbm,
    dual_hbm,
    trace_hbm,
    inv_hbm,
    sizes_ref,
    order_ref,
    lam_out,
    res_out,
    dir_out,
    lam_v,
    res_v,
    dir_v,
    dual_v,
    trace_v,
    inv_v,
    inv_pad,
    perm,
    own_rf,
    nb_rf,
    own_y,
    nb_y,
    windows,
    loads,
    parts,
    got,
    amps,
    norm_a,
    norm_b,
    in_sem,
    out_sem,
    send_sem,
    recv_sem,
):
    s = lax.axis_index("sub")
    g = lax.axis_index("grp")
    block = s // 4
    sl = s % 4
    place = sl * 4 + g

    copies_in = {}
    for k, (name, src, dst) in enumerate(
        (
            ("dir", dir_hbm, dir_v),
            ("trace", trace_hbm, trace_v),
            ("inv", inv_hbm, inv_v),
            ("dual", dual_hbm, dual_v),
            ("res", res_hbm, res_v),
            ("lam", lam_hbm, lam_v),
        )
    ):
        copies_in[name] = pltpu.make_async_copy(src, dst, in_sem.at[k])
        copies_in[name].start()

    across = (
        ((s + 63) % 64, g),
        ((s + 1) % 64, g),
        (s, (g + 3) % 4),
        (s, (g + 1) % 4),
    )

    def mate(step):
        other = (place + step) % MEMBERS
        return (block * 4 + other // 4, other % 4)

    def peer(step):
        other = (block + step) % MEMBERS
        return other, (other * 4 + sl, g)

    barrier = pltpu.get_barrier_semaphore()
    for target in across:
        pl.semaphore_signal(barrier, inc=1, device_id=target, device_id_type=MESH)
    for step in range(1, MEMBERS):
        pl.semaphore_signal(barrier, inc=1, device_id=mate(step), device_id_type=MESH)
        pl.semaphore_signal(barrier, inc=1, device_id=peer(step)[1], device_id_type=MESH)

    def send(src, dst, phase, target):
        pltpu.make_async_remote_copy(
            src_ref=src,
            dst_ref=dst,
            send_sem=send_sem.at[phase],
            recv_sem=recv_sem.at[phase],
            device_id=target,
            device_id_type=MESH,
        ).start()

    def wait_recv(ref, phase):
        pltpu.make_async_copy(ref, ref, recv_sem.at[phase]).wait()

    def wait_send(ref, phase):
        pltpu.make_async_copy(ref, ref, send_sem.at[phase]).wait()

    def limits(face):
        out = jnp.zeros_like(face)
        for f in range(4):
            out = jnp.where(face == f, sizes_ref[0, 0, f], out)
        return out

    lane = iota((1, WIDE), 1)
    face = face_at(lane, PAD)
    active_pad = (lane - face * PAD) < limits(face)
    sign_pad = jnp.where((face & 1) == 0, -1.0, 1.0)
    mask_pad = jnp.where(active_pad, sign_pad, 0.0)
    flat = iota((1, WIDTH), 1)
    flat_face = face_at(flat, FACE)
    active = (flat - flat_face * FACE) < limits(flat_face)

    order = order_ref[0]
    order = order + (PAD - FACE) * face_at(order, FACE)
    for f in range(4):
        hot = iota((PAD, WIDTH), 0) + f * PAD == order
        perm[f * PAD : (f + 1) * PAD, :] = jnp.where(hot, 1.0, 0.0).astype(BF16)

    copies_in["trace"].wait()
    trace = jnp.concatenate([trace_v[...], jnp.zeros((2, WIDTH), F32)], axis=0)
    high, low = split(trace)
    both = jnp.concatenate([high.astype(F32), low.astype(F32)], axis=0).astype(BF16)
    for f in range(4):
        got_rf = mm(both, perm[f * PAD : (f + 1) * PAD, :], NT)
        own_rf[f] = (got_rf[:8] + got_rf[8:]) * mask_pad[:, f * PAD : (f + 1) * PAD]
    copies_in["inv"].wait()
    inv_pad[...] = jnp.concatenate([inv_v[...], jnp.zeros((2, COARSE), F32)], axis=0)

    pl.semaphore_wait(barrier, 34)
    for f in range(4):
        send(own_rf.at[f], nb_rf.at[f ^ 1], 0, across[f])
    for b in range(MEMBERS):
        piece = inv_pad.at[:, window_start(b) : window_start(b) + WINDOW]

        @pl.when(block != b)
        def _():
            send(piece, windows.at[block], 1, (b * 4 + sl, g))

        @pl.when(block == b)
        def _():
            windows[b] = piece[...]

    copies_in["dir"].wait()
    direction = dir_v[...]
    gap = jnp.zeros((CASES, PAD - FACE), F32)
    spread = []
    for f in range(4):
        spread += [direction[:, f * FACE : (f + 1) * FACE], gap]
    spread = jnp.concatenate(spread, axis=1)
    spread = jnp.where(active_pad, spread * sign_pad, 0.0)
    high, low = split(spread)
    slots = mm(jnp.concatenate([high, low], axis=0), perm[...], NN)
    slots = slots[:CASES] + slots[CASES:]

    high, low = split(slots)
    both = jnp.concatenate([high, low], axis=0)
    copies_in["dual"].wait()
    pieces = []
    for k in range(0, WIDTH, 256):
        f_high, f_low = split(dual_v[k : min(k + 256, WIDTH), :])
        first = mm(both, f_high, NT)
        pieces.append(first[:CASES] + first[CASES:] + mm(high, f_low, NT))
    z = jnp.concatenate(pieces, axis=1)

    high, low = split(z)
    both = jnp.concatenate([high, low], axis=0)
    wait_recv(nb_rf, 0)
    own_load = jnp.zeros((8, 128), F32)
    for f in range(4):
        cut = slice(f * PAD, (f + 1) * PAD)
        y = mm(both, perm[cut, :], NT)
        y = (y[:CASES] + y[CASES:]) * mask_pad[:, cut]
        own_y[f] = y
        nb_rf[f] = jnp.where(active_pad[:, cut], nb_rf[f], 0.0)
        rf = jnp.concatenate([own_rf[f], nb_rf[f]], axis=0)
        r_high, r_low = split(rf)
        y_high, y_low = split(y)
        piece = mm(
            jnp.concatenate([r_high, r_low], axis=0), jnp.concatenate([y_high, y_low], axis=0), NT
        )
        piece = piece[:16] + piece[16:]
        piece = piece + pltpu.roll(piece, 64, 1)
        own_load = own_load + piece[:8]
        loads[place, 8 * (f + 1) : 8 * (f + 2), :] = piece[8:]

    copies_in["res"].wait()
    res = jnp.where(active, res_v[...], 0.0)
    rr_row = row_of(0.5 * jnp.sum(res * res, axis=1, keepdims=True))
    curv_row = row_of(jnp.sum(slots * z, axis=1, keepdims=True))
    row = iota((8, 128), 0)
    own_load = jnp.where(row == 6, rr_row, jnp.where(row == 7, curv_row, own_load))
    loads[place, 0:8, :] = own_load
    for step in range(1, MEMBERS):
        send(loads.at[place], loads.at[place], 2, mate(step))
    for f in range(4):
        send(own_y.at[f], nb_y.at[f ^ 1], 3, across[f])

    col = iota((1, 40 * MEMBERS), 1)
    unit = col >> 3
    mode = col & 7
    member = (unit * 205) >> 10
    group = unit - member * 5
    d_sub = jnp.where(group == 1, -1, jnp.where(group == 2, 1, 0))
    d_grp = jnp.where(group == 3, -1, jnp.where(group == 4, 1, 0))
    m_sub = block * 4 + (member >> 2) + d_sub
    m_grp = (member & 3) + d_grp
    start = jnp.clip(((96 * block + 104) // 128 - 1) * 128, 0, COARSE - WINDOW)
    source = (m_sub * 4 + m_grp) * MODES + mode - start
    source = jnp.where(mode < MODES, source, -1)
    pick = jnp.where(iota((WINDOW, 40 * MEMBERS), 0) == source, 1.0, 0.0).astype(BF16)
    wait_recv(windows.at[0 : MEMBERS - 1], 1)
    high, low = split(windows[...].reshape(MEMBERS * 8, WINDOW))
    piece = mm(jnp.concatenate([high, low], axis=0), pick, NN).astype(BF16)

    wait_recv(loads.at[0 : MEMBERS - 1], 2)
    every = loads[...]
    total = jnp.sum(every[:, 0:8, :], axis=0)
    flat_load = every.reshape(MEMBERS * 40, 128)
    high = flat_load.astype(BF16)
    low = (flat_load - high.astype(F32)).astype(BF16)
    both = jnp.where(iota((MEMBERS * 40, 128), 1) < 64, high.astype(F32), low.astype(F32)).astype(BF16)
    part = mm(piece, both, NN)
    part = part[:128] + part[128:]
    part = part + pltpu.roll(part, 64, 1)
    part = part.reshape(MEMBERS, 8, 128)
    parts[...] = part + jnp.where(row >= 6, total, 0.0)[None]
    for step in range(1, MEMBERS):
        other, target = peer(step)
        send(parts.at[other], got.at[block], 4, target)
    got[block] = parts[block]
    wait_recv(got.at[0 : MEMBERS - 1], 4)
    amp = jnp.sum(got[...], axis=0)
    amps[0] = amp
    for f in range(4):
        send(amps.at[0], amps.at[1 + (f ^ 1)], 5, across[f])

    rr = column_of(amp[6:7, :])
    curvature = column_of(amp[7:8, :])
    step_size = rr / curvature
    dirn = jnp.where(active, dir_v[...], 0.0)
    copies_in["lam"].wait()
    lam_v[...] = jnp.where(active, lam_v[...], 0.0) + step_size * dirn
    lam_copy = pltpu.make_async_copy(lam_v, lam_out, out_sem.at[0])
    lam_copy.start()

    wait_recv(nb_y, 3)
    wait_recv(amps.at[1:5], 5)
    spread = []
    for f in range(4):
        cut = slice(f * PAD, (f + 1) * PAD)
        a_high, a_low = split(jnp.concatenate([amp, amps[1 + f]], axis=0))
        r_high, r_low = split(jnp.concatenate([own_rf[f], nb_rf[f]], axis=0))
        back = mm(
            jnp.concatenate([a_high, a_low, a_high, a_low], axis=0),
            jnp.concatenate([r_high, r_high, r_low, r_low], axis=0),
            TN,
        )
        image = own_y[f] + jnp.where(active_pad[:, cut], nb_y[f], 0.0)
        spread.append((image - back[:CASES])[:, :FACE])
    projected = jnp.concatenate(spread, axis=1)
    res = jnp.where(active, res_v[...], 0.0) - step_size * projected
    res_v[...] = res
    res_copy = pltpu.make_async_copy(res_v, res_out, out_sem.at[1])
    res_copy.start()

    next_row = row_of(0.5 * jnp.sum(res * res, axis=1, keepdims=True))
    norm_a[place] = jnp.broadcast_to(next_row, (8, 128))
    for step in range(1, MEMBERS):
        send(norm_a.at[place], norm_a.at[place], 6, mate(step))
    wait_recv(norm_a.at[0 : MEMBERS - 1], 6)
    norm_b[block] = jnp.sum(norm_a[...], axis=0)
    for step in range(1, MEMBERS):
        send(norm_b.at[block], norm_b.at[block], 7, peer(step)[1])
    wait_recv(norm_b.at[0 : MEMBERS - 1], 7)
    rr_next = column_of(jnp.sum(norm_b[...], axis=0)[0:1, :])
    dir_v[...] = res + (rr_next / rr) * dirn
    dir_copy = pltpu.make_async_copy(dir_v, dir_out, out_sem.at[2])
    dir_copy.start()

    wait_send(own_rf, 0)
    wait_send(windows.at[0 : MEMBERS - 1], 1)
    wait_send(loads.at[0 : MEMBERS - 1], 2)
    wait_send(own_y, 3)
    wait_send(parts.at[0 : MEMBERS - 1], 4)
    wait_send(amps.at[1:5], 5)
    wait_send(norm_a.at[0 : MEMBERS - 1], 6)
    wait_send(norm_b.at[0 : MEMBERS - 1], 7)
    lam_copy.wait()
    res_copy.wait()
    dir_copy.wait()


def on_device(
    multipliers,
    residual,
    direction,
    dual_operator,
    rigid_trace,
    coarse_inverse,
    face_sizes,
    slot_order,
):
    field = jax.ShapeDtypeStruct((CASES, WIDTH), F32)
    anywhere = pl.BlockSpec(memory_space=pl.ANY)
    outs = pl.pallas_call(
        kernel,
        out_shape=(field, field, field),
        in_specs=[anywhere] * 6
        + [pl.BlockSpec(memory_space=pltpu.SMEM), pl.BlockSpec(memory_space=pltpu.VMEM)],
        out_specs=(anywhere, anywhere, anywhere),
        scratch_shapes=[
            pltpu.VMEM((CASES, WIDTH), F32),
            pltpu.VMEM((CASES, WIDTH), F32),
            pltpu.VMEM((CASES, WIDTH), F32),
            pltpu.VMEM((WIDTH, WIDTH), F32),
            pltpu.VMEM((MODES, WIDTH), F32),
            pltpu.VMEM((MODES, COARSE), F32),
            pltpu.VMEM((8, COARSE), F32),
            pltpu.VMEM((WIDE, WIDTH), BF16),
            pltpu.VMEM((4, 8, PAD), F32),
            pltpu.VMEM((4, 8, PAD), F32),
            pltpu.VMEM((4, CASES, PAD), F32),
            pltpu.VMEM((4, CASES, PAD), F32),
            pltpu.VMEM((MEMBERS, 8, WINDOW), F32),
            pltpu.VMEM((MEMBERS, 40, 128), F32),
            pltpu.VMEM((MEMBERS, 8, 128), F32),
            pltpu.VMEM((MEMBERS, 8, 128), F32),
            pltpu.VMEM((5, 8, 128), F32),
            pltpu.VMEM((MEMBERS, 8, 128), F32),
            pltpu.VMEM((MEMBERS, 8, 128), F32),
            pltpu.SemaphoreType.DMA((6,)),
            pltpu.SemaphoreType.DMA((3,)),
            pltpu.SemaphoreType.DMA((8,)),
            pltpu.SemaphoreType.DMA((8,)),
        ],
        compiler_params=pltpu.CompilerParams(
            collective_id=0, has_side_effects=True, vmem_limit_bytes=48 * 1024 * 1024
        ),
    )(
        multipliers.reshape(CASES, WIDTH),
        residual.reshape(CASES, WIDTH),
        direction.reshape(CASES, WIDTH),
        dual_operator.reshape(WIDTH, WIDTH),
        rigid_trace.reshape(MODES, WIDTH),
        coarse_inverse,
        face_sizes,
        slot_order,
    )
    return tuple(x[None, None] for x in outs)


def solution(mesh):
    wide = P("sub", "grp", None, None)
    return jax.shard_map(
        on_device,
        mesh=mesh,
        in_specs=(wide, wide, wide, wide, wide, P(("sub", "grp"), None), P("sub", "grp", None), P("sub", "grp", None)),
        out_specs=(wide, wide, wide),
        check_vma=False,
    )
```

```python
import functools

import jax
import jax.numpy as jnp
from jax import lax
from jax.experimental import pallas as pl
from jax.experimental.pallas import tpu as pltpu
from jax.sharding import PartitionSpec as P

MESH = pl.DeviceIdType.MESH
F32 = jnp.float32
BF16 = jnp.bfloat16
NN = (((1,), (0,)), ((), ()))
NT = (((1,), (1,)), ((), ()))
TN = (((0,), (0,)), ((), ()))

CASES = 64
WIDTH = 1200
FACE = 300
PAD = 384
WIDE = 4 * PAD
MODES = 6
COARSE = 1536
WINDOW = 256
MEMBERS = 16


def split(x):
    high = x.astype(BF16)
    return high, (x - high.astype(F32)).astype(BF16)


def mm(a, b, dims):
    return lax.dot_general(a, b, dims, preferred_element_type=F32)


def iota(shape, dim):
    return lax.broadcasted_iota(jnp.int32, shape, dim)


def face_at(lane, step):
    one = jnp.int32(1)
    zero = jnp.int32(0)
    return (
        jnp.where(lane >= step, one, zero)
        + jnp.where(lane >= 2 * step, one, zero)
        + jnp.where(lane >= 3 * step, one, zero)
    )


def row_of(column):
    eye = iota((CASES, 128), 0) == iota((CASES, 128), 1)
    return jnp.sum(jnp.where(eye, column, 0.0), axis=0, keepdims=True)


def column_of(row):
    eye = iota((CASES, 128), 0) == iota((CASES, 128), 1)
    return jnp.sum(jnp.where(eye, row, 0.0), axis=1, keepdims=True)


def window_start(block):
    return min(max(((96 * block - 24) // 128) * 128, 0), COARSE - WINDOW)


def kernel(
    res_hbm,
    dir_hbm,
    dual_hbm,
    trace_hbm,
    inv_hbm,
    sizes_hbm,
    order_hbm,
    proj_out,
    coef_out,
    proj_v,
    res_v,
    dir_v,
    dual_v,
    trace_v,
    inv_v,
    order_ref,
    sizes_ref,
    inv_pad,
    perm,
    own_rf,
    nb_rf,
    own_y,
    nb_y,
    windows,
    loads,
    parts,
    got,
    amps,
    norm_a,
    norm_b,
    in_sem,
    out_sem,
    send_sem,
    recv_sem,
):
    s = lax.axis_index("sub")
    g = lax.axis_index("grp")
    block = s // 4
    sl = s % 4
    place = sl * 4 + g

    copies_in = {}
    for k, (name, src, dst) in enumerate(
        (
            ("sizes", sizes_hbm, sizes_ref),
            ("order", order_hbm, order_ref),
            ("trace", trace_hbm, trace_v),
            ("dir", dir_hbm, dir_v),
            ("inv", inv_hbm, inv_v),
            ("dual", dual_hbm, dual_v),
            ("res", res_hbm, res_v),
        )
    ):
        copies_in[name] = pltpu.make_async_copy(src, dst, in_sem.at[k])
        copies_in[name].start()

    across = (
        ((s + 63) % 64, g),
        ((s + 1) % 64, g),
        (s, (g + 3) % 4),
        (s, (g + 1) % 4),
    )

    def mate(step):
        other = (place + step) % MEMBERS
        return (block * 4 + other // 4, other % 4)

    def peer(step):
        other = (block + step) % MEMBERS
        return other, (other * 4 + sl, g)

    barrier = pltpu.get_barrier_semaphore()
    for target in across:
        pl.semaphore_signal(barrier, inc=1, device_id=target, device_id_type=MESH)
    for step in range(1, MEMBERS):
        pl.semaphore_signal(barrier, inc=1, device_id=mate(step), device_id_type=MESH)
        pl.semaphore_signal(barrier, inc=1, device_id=peer(step)[1], device_id_type=MESH)

    def send(src, dst, phase, target):
        pltpu.make_async_remote_copy(
            src_ref=src,
            dst_ref=dst,
            send_sem=send_sem.at[phase],
            recv_sem=recv_sem.at[phase],
            device_id=target,
            device_id_type=MESH,
        ).start()

    def wait_recv(ref, phase):
        pltpu.make_async_copy(ref, ref, recv_sem.at[phase]).wait()

    def wait_send(ref, phase):
        pltpu.make_async_copy(ref, ref, send_sem.at[phase]).wait()

    def greeted():
        pl.semaphore_wait(barrier, 34)
        for f in range(4):
            send(own_rf.at[f], nb_rf.at[f ^ 1], 0, across[f])
        for b in range(MEMBERS):
            piece = inv_pad.at[:, window_start(b) : window_start(b) + WINDOW]

            @pl.when(block != b)
            def _():
                send(piece, windows.at[block], 1, (b * 4 + sl, g))

            @pl.when(block == b)
            def _():
                windows[b] = piece[...]

    copies_in["sizes"].wait()
    copies_in["order"].wait()

    def limits(face):
        out = jnp.zeros_like(face)
        for f in range(4):
            out = jnp.where(face == f, sizes_ref[0, 0, f], out)
        return out

    lane = iota((1, WIDE), 1)
    face = face_at(lane, PAD)
    active_pad = (lane - face * PAD) < limits(face)
    sign_pad = jnp.where((face & 1) == 0, -1.0, 1.0)
    mask_pad = jnp.where(active_pad, sign_pad, 0.0)
    flat = iota((1, WIDTH), 1)
    flat_face = face_at(flat, FACE)
    active = (flat - flat_face * FACE) < limits(flat_face)

    order = order_ref[0]
    order = order + (PAD - FACE) * face_at(order, FACE)
    for f in range(4):
        hot = iota((PAD, WIDTH), 0) + f * PAD == order
        perm[f * PAD : (f + 1) * PAD, :] = jnp.where(hot, 1.0, 0.0).astype(BF16)

    copies_in["trace"].wait()
    trace = jnp.concatenate([trace_v[...].reshape(MODES, WIDTH), jnp.zeros((2, WIDTH), F32)], axis=0)
    high, low = split(trace)
    both = jnp.concatenate([high.astype(F32), low.astype(F32)], axis=0).astype(BF16)
    for f in range(4):
        got_rf = mm(both, perm[f * PAD : (f + 1) * PAD, :], NT)
        own_rf[f] = (got_rf[:8] + got_rf[8:]) * mask_pad[:, f * PAD : (f + 1) * PAD]
    copies_in["inv"].wait()
    inv_pad[...] = jnp.concatenate([inv_v[...], jnp.zeros((2, COARSE), F32)], axis=0)

    copies_in["dir"].wait()
    direction = dir_v[...]
    gap = jnp.zeros((CASES, PAD - FACE), F32)
    spread = []
    for f in range(4):
        spread += [direction[:, f * FACE : (f + 1) * FACE], gap]
    spread = jnp.concatenate(spread, axis=1)
    spread = jnp.where(active_pad, spread * sign_pad, 0.0)
    high, low = split(spread)
    slots = mm(jnp.concatenate([high, low], axis=0), perm[...], NN)
    slots = slots[:CASES] + slots[CASES:]

    high, low = split(slots)
    both = jnp.concatenate([high, low], axis=0)
    copies_in["dual"].wait()
    pieces = []
    for k in range(0, WIDTH, 256):
        if k == 512:
            greeted()
        f_high, f_low = split(dual_v[k : min(k + 256, WIDTH), :])
        first = mm(both, f_high, NT)
        pieces.append(first[:CASES] + first[CASES:] + mm(high, f_low, NT))
    z = jnp.concatenate(pieces, axis=1)

    high, low = split(z)
    both = jnp.concatenate([high, low], axis=0)
    for f in range(4):
        cut = slice(f * PAD, (f + 1) * PAD)
        y = mm(both, perm[cut, :], NT)
        own_y[f] = (y[:CASES] + y[CASES:]) * mask_pad[:, cut]
    wait_recv(nb_rf, 0)
    own_load = jnp.zeros((8, 128), F32)
    nb_load = []
    for f in range(4):
        cut = slice(f * PAD, (f + 1) * PAD)
        nb_rf[f] = jnp.where(active_pad[:, cut], nb_rf[f], 0.0)
        r_high, r_low = split(jnp.concatenate([own_rf[f], nb_rf[f]], axis=0))
        y_high, y_low = split(own_y[f])
        piece = mm(
            jnp.concatenate([r_high, r_low], axis=0), jnp.concatenate([y_high, y_low], axis=0), NT
        )
        piece = piece[:16] + piece[16:]
        piece = piece + pltpu.roll(piece, 64, 1)
        own_load = own_load + piece[:8]
        nb_load.append(piece[8:])
    copies_in["res"].wait()
    res = jnp.where(active, res_v[...], 0.0)
    rr_row = row_of(0.5 * jnp.sum(res * res, axis=1, keepdims=True))
    curv_row = row_of(jnp.sum(slots * z, axis=1, keepdims=True))
    row = iota((8, 128), 0)
    left = iota((8, 128), 1) < 64
    own_load = jnp.where(row == 6, rr_row, jnp.where(row == 7, curv_row, own_load))
    for f in range(3):
        moved = pltpu.roll(nb_load[3], 6 - 2 * f, 0)
        nb_load[f] = jnp.where(row < MODES, nb_load[f], moved)
    loads[place, 0:8, :] = jnp.where(left, own_load, nb_load[0])
    loads[place, 8:16, :] = jnp.where(left, nb_load[1], nb_load[2])
    for step in range(1, MEMBERS):
        send(loads.at[place], loads.at[place], 2, mate(step))
    for f in range(4):
        send(own_y.at[f], nb_y.at[f ^ 1], 3, across[f])

    col = iota((1, 2 * WINDOW), 1)
    mode = col & 7
    tile = 2 * ((col >> 3) & 1) + (col >> 8)
    member = (col >> 4) & 15
    spare = (mode >= MODES) & (tile > 0)
    group = jnp.where(spare, 4, tile)
    mode = jnp.where(spare, 2 * (tile - 1) + mode - MODES, mode)
    d_sub = jnp.where(group == 1, -1, jnp.where(group == 2, 1, 0))
    d_grp = jnp.where(group == 3, -1, jnp.where(group == 4, 1, 0))
    m_sub = block * 4 + (member >> 2) + d_sub
    m_grp = (member & 3) + d_grp
    start = jnp.clip(((96 * block + 104) // 128 - 1) * 128, 0, COARSE - WINDOW)
    source = (m_sub * 4 + m_grp) * MODES + mode - start
    source = jnp.where(mode < MODES, source, -1)
    pick = jnp.where(iota((WINDOW, 2 * WINDOW), 0) == source, 1.0, 0.0).astype(BF16)
    wait_recv(windows.at[0 : MEMBERS - 1], 1)
    high, low = split(windows[...].reshape(MEMBERS * 8, WINDOW))
    piece = mm(jnp.concatenate([high, low], axis=0), pick, NN).astype(BF16)
    piece = jnp.concatenate([piece[:, :WINDOW], piece[:, WINDOW:]], axis=0)

    wait_recv(loads.at[0 : MEMBERS - 1], 2)
    every = loads[...]
    total = jnp.sum(every[:, 0:8, :], axis=0)
    total = jnp.where(left, total, pltpu.roll(total, 64, 1))
    high, low = split(every.reshape(MEMBERS * 16, 128))
    part = mm(piece, jnp.concatenate([high, low], axis=1), NN)
    part = part[:, :128] + part[:, 128:]
    part = jnp.where(
        iota((128, 128), 1) < 64, part[:128] + part[128:256], part[256:384] + part[384:]
    )
    part = part + pltpu.roll(part, 64, 1)
    part = part.reshape(MEMBERS, 8, 128) + jnp.where(row >= MODES, total, 0.0)[None]
    parts[...] = jnp.where(left[None], part, pltpu.roll(part, 4, 1))[:, 0:4, :]
    for step in range(1, MEMBERS):
        other, target = peer(step)
        send(parts.at[other], got.at[block], 4, target)
    got[block] = parts[block]
    wait_recv(got.at[0 : MEMBERS - 1], 4)
    amp = jnp.sum(got[...], axis=0)
    amp = jnp.concatenate([amp, pltpu.roll(amp, 64, 1)], axis=0)
    amp = jnp.where(left, amp, pltpu.roll(amp, 64, 1))
    amps[0] = amp
    for f in range(4):
        send(amps.at[0], amps.at[1 + (f ^ 1)], 5, across[f])

    rr = column_of(amp[6:7, :])
    curvature = column_of(amp[7:8, :])
    step_size = rr / curvature
    wait_recv(nb_y, 3)
    wait_recv(amps.at[1:5], 5)
    spread = []
    for f in range(4):
        cut = slice(f * PAD, (f + 1) * PAD)
        a_high, a_low = split(jnp.concatenate([amp, amps[1 + f]], axis=0))
        r_high, r_low = split(jnp.concatenate([own_rf[f], nb_rf[f]], axis=0))
        back = mm(
            jnp.concatenate([a_high, a_low, a_high, a_low], axis=0),
            jnp.concatenate([r_high, r_high, r_low, r_low], axis=0),
            TN,
        )
        image = own_y[f] + jnp.where(active_pad[:, cut], nb_y[f], 0.0)
        spread.append((image - back[:CASES])[:, :FACE])
    projected = jnp.concatenate(spread, axis=1)
    proj_v[...] = projected
    proj_copy = pltpu.make_async_copy(proj_v, proj_out, out_sem.at[0])
    proj_copy.start()
    res = jnp.where(active, res_v[...], 0.0) - step_size * projected

    next_row = row_of(0.5 * jnp.sum(res * res, axis=1, keepdims=True))
    norm_a[place] = next_row
    for step in range(1, MEMBERS):
        send(norm_a.at[place], norm_a.at[place], 6, mate(step))
    wait_recv(norm_a.at[0 : MEMBERS - 1], 6)
    norm_b[block] = jnp.sum(norm_a[...], axis=0)
    for step in range(1, MEMBERS):
        send(norm_b.at[block], norm_b.at[block], 7, peer(step)[1])
    wait_recv(norm_b.at[0 : MEMBERS - 1], 7)
    rr_next = column_of(jnp.sum(norm_b[...], axis=0))
    coef_out[...] = jnp.where(iota((CASES, 128), 1) < 64, step_size, rr_next / rr)

    wait_send(own_rf, 0)
    wait_send(windows.at[0 : MEMBERS - 1], 1)
    wait_send(loads.at[0 : MEMBERS - 1], 2)
    wait_send(own_y, 3)
    wait_send(parts.at[0 : MEMBERS - 1], 4)
    wait_send(amps.at[1:5], 5)
    wait_send(norm_a.at[0 : MEMBERS - 1], 6)
    wait_send(norm_b.at[0 : MEMBERS - 1], 7)
    proj_copy.wait()


def update(
    lam_hbm,
    res_hbm,
    dir_hbm,
    proj_hbm,
    coef_hbm,
    sizes_hbm,
    lam_out,
    res_out,
    dir_out,
    proj_v,
    coef_v,
    sizes_ref,
    lam_v,
    res_v,
    dir_v,
    sem,
):
    ins = [
        pltpu.make_async_copy(src, dst, sem.at[k])
        for k, (src, dst) in enumerate(
            (
                (sizes_hbm, sizes_ref),
                (dir_hbm, dir_v),
                (lam_hbm, lam_v),
                (coef_hbm, coef_v),
                (res_hbm, res_v),
                (proj_hbm, proj_v),
            )
        )
    ]
    for copy in ins:
        copy.start()
    outs = [
        pltpu.make_async_copy(src, dst, sem.at[6 + k])
        for k, (src, dst) in enumerate(((lam_v, lam_out), (res_v, res_out), (dir_v, dir_out)))
    ]
    ins[0].wait()
    flat = iota((1, WIDTH), 1)
    face = face_at(flat, FACE)
    limit = jnp.zeros_like(face)
    for f in range(4):
        limit = jnp.where(face == f, sizes_ref[0, 0, f], limit)
    active = (flat - face * FACE) < limit
    ins[1].wait()
    dirn = jnp.where(active, dir_v[...], 0.0)
    ins[2].wait()
    ins[3].wait()
    coef = coef_v[...]
    step_size = coef[:, 0:1]
    ratio = coef[:, 64:65]
    lam_v[...] = jnp.where(active, lam_v[...], 0.0) + step_size * dirn
    outs[0].start()
    ins[4].wait()
    ins[5].wait()
    res = jnp.where(active, res_v[...], 0.0) - step_size * proj_v[...]
    res_v[...] = res
    outs[1].start()
    dir_v[...] = res + ratio * dirn
    outs[2].start()
    for copy in outs:
        copy.wait()


def on_device(
    multipliers,
    residual,
    direction,
    dual_operator,
    rigid_trace,
    coarse_inverse,
    face_sizes,
    slot_order,
):
    field = jax.ShapeDtypeStruct((CASES, WIDTH), F32)
    hbm = pl.BlockSpec(memory_space=pltpu.HBM)
    vmem = pl.BlockSpec(memory_space=pltpu.VMEM)
    projected, coef = pl.pallas_call(
        kernel,
        out_shape=(
            field,
            jax.ShapeDtypeStruct((CASES, 128), F32),
        ),
        in_specs=[hbm] * 7,
        out_specs=[hbm, vmem],
        scratch_shapes=[
            pltpu.VMEM((CASES, WIDTH), F32),
            pltpu.VMEM((CASES, WIDTH), F32),
            pltpu.VMEM((CASES, WIDTH), F32),
            pltpu.VMEM((WIDTH, WIDTH), F32),
            pltpu.VMEM((MODES, 1, WIDTH), F32),
            pltpu.VMEM((MODES, COARSE), F32),
            pltpu.VMEM((1, 1, WIDTH), jnp.int32),
            pltpu.SMEM((1, 1, 4), jnp.int32),
            pltpu.VMEM((8, COARSE), F32),
            pltpu.VMEM((WIDE, WIDTH), BF16),
            pltpu.VMEM((4, 8, PAD), F32),
            pltpu.VMEM((4, 8, PAD), F32),
            pltpu.VMEM((4, CASES, PAD), F32),
            pltpu.VMEM((4, CASES, PAD), F32),
            pltpu.VMEM((MEMBERS, 8, WINDOW), F32),
            pltpu.VMEM((MEMBERS, 16, 128), F32),
            pltpu.VMEM((MEMBERS, 4, 128), F32),
            pltpu.VMEM((MEMBERS, 4, 128), F32),
            pltpu.VMEM((5, 8, 128), F32),
            pltpu.VMEM((MEMBERS, 1, 128), F32),
            pltpu.VMEM((MEMBERS, 1, 128), F32),
            pltpu.SemaphoreType.DMA((7,)),
            pltpu.SemaphoreType.DMA((1,)),
            pltpu.SemaphoreType.DMA((8,)),
            pltpu.SemaphoreType.DMA((8,)),
        ],
        compiler_params=pltpu.CompilerParams(
            collective_id=0, has_side_effects=True, vmem_limit_bytes=62 * 1024 * 1024
        ),
    )(
        residual.reshape(CASES, WIDTH),
        direction.reshape(CASES, WIDTH),
        dual_operator.reshape(WIDTH, WIDTH),
        rigid_trace.transpose(0, 2, 1, 3).reshape(MODES, 1, WIDTH),
        coarse_inverse,
        face_sizes,
        slot_order,
    )
    outs = pl.pallas_call(
        update,
        out_shape=(field, field, field),
        in_specs=[hbm] * 6,
        out_specs=[hbm, hbm, hbm],
        scratch_shapes=[
            pltpu.VMEM((CASES, WIDTH), F32),
            pltpu.VMEM((CASES, 128), F32),
            pltpu.SMEM((1, 1, 4), jnp.int32),
            pltpu.VMEM((CASES, WIDTH), F32),
            pltpu.VMEM((CASES, WIDTH), F32),
            pltpu.VMEM((CASES, WIDTH), F32),
            pltpu.SemaphoreType.DMA((9,)),
        ],
        compiler_params=pltpu.CompilerParams(vmem_limit_bytes=62 * 1024 * 1024),
    )(
        multipliers.reshape(CASES, WIDTH),
        residual.reshape(CASES, WIDTH),
        direction.reshape(CASES, WIDTH),
        projected,
        coef,
        face_sizes,
    )
    return tuple(x[None, None] for x in outs)


def solution(mesh):
    wide = P("sub", "grp", None, None)
    return jax.shard_map(
        on_device,
        mesh=mesh,
        in_specs=(wide, wide, wide, wide, wide, P(("sub", "grp"), None), P("sub", "grp", None), P("sub", "grp", None)),
        out_specs=(wide, wide, wide),
        check_vma=False,
    )
```

```python
import functools

import jax
import jax.numpy as jnp
from jax import lax
from jax.experimental import pallas as pl
from jax.experimental.pallas import tpu as pltpu
from jax.sharding import PartitionSpec as P

MESH = pl.DeviceIdType.MESH
F32 = jnp.float32
BF16 = jnp.bfloat16
NN = (((1,), (0,)), ((), ()))
NT = (((1,), (1,)), ((), ()))
TN = (((0,), (0,)), ((), ()))

CASES = 64
WIDTH = 1200
FACE = 300
PAD = 384
WIDE = 4 * PAD
MODES = 6
COARSE = 1536
PAIRS = 32
MATES = 8


def split(x):
    high = x.astype(BF16)
    return high, (x - high.astype(F32)).astype(BF16)


def mm(a, b, dims):
    return lax.dot_general(a, b, dims, preferred_element_type=F32)


def iota(shape, dim):
    return lax.broadcasted_iota(jnp.int32, shape, dim)


def face_at(lane, step):
    one = jnp.int32(1)
    zero = jnp.int32(0)
    return (
        jnp.where(lane >= step, one, zero)
        + jnp.where(lane >= 2 * step, one, zero)
        + jnp.where(lane >= 3 * step, one, zero)
    )


def row_of(column):
    eye = iota((CASES, 128), 0) == iota((CASES, 128), 1)
    return jnp.sum(jnp.where(eye, column, 0.0), axis=0, keepdims=True)


def column_of(row):
    eye = iota((CASES, 128), 0) == iota((CASES, 128), 1)
    return jnp.sum(jnp.where(eye, row, 0.0), axis=1, keepdims=True)


def packed(tile):
    left = iota((8, 128), 1) < 64
    return jnp.where(left, tile, pltpu.roll(tile, 4, 0))[0:4]


def unpacked(half):
    return jnp.concatenate([half, pltpu.roll(half, 64, half.ndim - 1)], axis=half.ndim - 2)


def doubled(x):
    return jnp.where(iota(x.shape, 1) < 64, x, pltpu.roll(x, 64, 1))


def lanes_split(x):
    high = x.astype(BF16).astype(F32)
    return jnp.where(iota(x.shape, 1) < 64, high, x - high).astype(BF16)


def both_sides(x):
    other = pltpu.roll(x, 64, 1)
    left = iota(x.shape, 1) < 64
    return jnp.concatenate(
        [lanes_split(jnp.where(left, x, other)), lanes_split(jnp.where(left, other, x))], axis=0
    )


def summed(x):
    return x + pltpu.roll(x, 64, 1)


def kernel(
    res_hbm,
    dir_hbm,
    dual_hbm,
    trace_hbm,
    inv_hbm,
    sizes_hbm,
    order_hbm,
    res_out,
    coef_out,
    next_v,
    res_v,
    dir_v,
    dual_v,
    trace_v,
    inv_v,
    order_ref,
    sizes_ref,
    perm,
    halves,
    own_rf,
    nb_rf,
    res_pad,
    own_y,
    nb_y,
    rows_out,
    rows_in,
    loads,
    parts,
    got,
    grams,
    amps,
    norms,
    in_sem,
    out_sem,
    send_sem,
    recv_sem,
):
    s = lax.axis_index("sub")
    g = lax.axis_index("grp")
    pair = s // 2
    core = s % 2
    place = core * 4 + g

    copies_in = {}
    for k, (name, src, dst) in enumerate(
        (
            ("sizes", sizes_hbm, sizes_ref),
            ("order", order_hbm, order_ref),
            ("trace", trace_hbm, trace_v),
            ("dir", dir_hbm, dir_v),
            ("inv", inv_hbm, inv_v),
            ("dual", dual_hbm, dual_v),
            ("res", res_hbm, res_v),
        )
    ):
        copies_in[name] = pltpu.make_async_copy(src, dst, in_sem.at[k])
        copies_in[name].start()

    across = (
        ((s + 63) % 64, g),
        ((s + 1) % 64, g),
        (s, (g + 3) % 4),
        (s, (g + 1) % 4),
    )

    def mate(step):
        other = (place + step) % MATES
        return (pair * 2 + other // 4, other % 4)

    def peer(step):
        other = (pair + step) % PAIRS
        return other, (other * 2 + core, g)

    beside = (pair + 2 * core - 1 + PAIRS) % PAIRS

    barrier = pltpu.get_barrier_semaphore()
    for step in range(1, PAIRS):
        pl.semaphore_signal(barrier, inc=1, device_id=peer(step)[1], device_id_type=MESH)
    for other in range(4):
        for target in ((2 * pair + 63) % 64, other), ((2 * pair + 2) % 64, other):
            pl.semaphore_signal(barrier, inc=1, device_id=target, device_id_type=MESH)
    for step in range(1, MATES):
        pl.semaphore_signal(barrier, inc=1, device_id=mate(step), device_id_type=MESH)

    def send(src, dst, phase, target):
        pltpu.make_async_remote_copy(
            src_ref=src,
            dst_ref=dst,
            send_sem=send_sem.at[phase],
            recv_sem=recv_sem.at[phase],
            device_id=target,
            device_id_type=MESH,
        ).start()

    def wait_recv(ref, phase):
        pltpu.make_async_copy(ref, ref, recv_sem.at[phase]).wait()

    def wait_send(ref, phase):
        pltpu.make_async_copy(ref, ref, send_sem.at[phase]).wait()

    def greeted():
        pl.semaphore_wait(barrier, PAIRS - 1 + 8 + MATES - 1)
        for f in range(4):
            send(own_rf.at[f], nb_rf.at[f ^ 1], 0, across[f])
        for step in range(1, PAIRS):
            other, target = peer(step)
            send(rows_out.at[other], rows_in.at[pair], 1, target)

    copies_in["sizes"].wait()
    copies_in["order"].wait()

    def limits(face):
        out = jnp.zeros_like(face)
        for f in range(4):
            out = jnp.where(face == f, sizes_ref[0, 0, f], out)
        return out

    lane = iota((1, WIDE), 1)
    face = face_at(lane, PAD)
    active_pad = (lane - face * PAD) < limits(face)
    sign_pad = jnp.where((face & 1) == 0, -1.0, 1.0)
    mask_pad = jnp.where(active_pad, sign_pad, 0.0)
    left = iota((8, 128), 1) < 64
    row = iota((8, 128), 0)

    order = order_ref[0]
    order = order + (PAD - FACE) * face_at(order, FACE)
    line = lax.broadcasted_iota(jnp.int16, (PAD, WIDTH), 0)
    ones = jnp.ones((PAD, WIDTH), BF16)
    for f in range(4):
        hot = line == jnp.broadcast_to((order - f * PAD).astype(jnp.int16), (PAD, WIDTH))
        perm[f * PAD : (f + 1) * PAD, :] = jnp.where(hot, ones, jnp.zeros_like(ones))

    copies_in["trace"].wait()
    trace = jnp.concatenate([trace_v[...].reshape(MODES, WIDTH), jnp.zeros((2, WIDTH), F32)], axis=0)
    high, low = split(trace)
    both = jnp.concatenate([high.astype(F32), low.astype(F32)], axis=0).astype(BF16)
    for f in range(4):
        got_rf = mm(both, perm[f * PAD : (f + 1) * PAD, :], NT)
        own_rf[f] = (got_rf[:8] + got_rf[8:]) * mask_pad[:, f * PAD : (f + 1) * PAD]

    copies_in["inv"].wait()
    rows = jnp.concatenate([inv_v[...], jnp.zeros((2, COARSE), F32)], axis=0)
    rows = jnp.concatenate([jnp.zeros((8, 24), F32), rows, jnp.zeros((8, 104), F32)], axis=1)
    for p in range(PAIRS):
        rows_out[p] = rows[:, 48 * p : 48 * p + 128]

    def padded(x):
        gap = jnp.zeros((CASES, PAD - FACE), F32)
        spread = []
        for f in range(4):
            spread += [x[:, f * FACE : (f + 1) * FACE], gap]
        return jnp.where(active_pad, jnp.concatenate(spread, axis=1), 0.0)

    copies_in["dir"].wait()
    dir_pad = padded(dir_v[...])
    dir_high, dir_low = split(dir_pad * sign_pad)
    slots = mm(jnp.concatenate([dir_high, dir_low], axis=0), perm[...], NN)
    slots = slots[:CASES] + slots[CASES:]

    high, low = split(slots)
    both = jnp.concatenate([high, low], axis=0)
    copies_in["dual"].wait()
    for k in range(0, WIDTH, 240):
        if k == 480:
            greeted()
        f_high, f_low = split(dual_v[k : k + 240, :])
        z_high, z_low = split(mm(f_high, both, NT) + mm(f_low, both, NT))
        halves[k : k + 240, 0:128] = z_high
        halves[k : k + 240, 128:256] = z_low

    ys = []
    for f in range(4):
        y = mm(perm[f * PAD : (f + 1) * PAD, :], halves[...], NN)
        ys.append(y[:, :128] + y[:, 128:])
    copies_in["res"].wait()
    flat = iota((1, WIDTH), 1)
    flat_face = face_at(flat, FACE)
    active = (flat - flat_face * FACE) < limits(flat_face)
    res = jnp.where(active, res_v[...], 0.0)
    rr_row = row_of(0.5 * jnp.sum(res * res, axis=1, keepdims=True))
    wait_recv(nb_rf, 0)
    own_load = jnp.zeros((8, 128), F32)
    curvature = jnp.zeros((CASES, 128), F32)
    nb_load = []
    for f in range(4):
        cut = slice(f * PAD, (f + 1) * PAD)
        nb_rf[f] = jnp.where(active_pad[:, cut], nb_rf[f], 0.0)
        r_high, r_low = split(jnp.concatenate([own_rf[f], nb_rf[f]], axis=0))
        y_high, y_low = split(ys[f])
        piece = mm(
            jnp.concatenate([r_high, r_low, dir_high[:, cut], dir_low[:, cut]], axis=0),
            jnp.concatenate([y_high, y_low], axis=1),
            NN,
        )
        piece = piece[:, :128] + piece[:, 128:]
        curvature = curvature + piece[32 : 32 + CASES] + piece[32 + CASES :]
        piece = piece[:16] + piece[16:32]
        if not f & 1:
            piece = -piece
        own_load = own_load + piece[:8]
        nb_load.append(summed(piece[8:]))
    own_load = summed(own_load)
    diagonal = (iota((CASES, 128), 1) & 63) == iota((CASES, 128), 0)
    curv_row = summed(jnp.sum(jnp.where(diagonal, curvature, 0.0), axis=0, keepdims=True))
    own_load = jnp.where(row == 6, rr_row, jnp.where(row == 7, curv_row, own_load))
    for f in range(3):
        moved = pltpu.roll(nb_load[3], 6 - 2 * f, 0)
        nb_load[f] = jnp.where(row < MODES, nb_load[f], moved)
    loads[place, 0:8, :] = jnp.where(left, own_load, nb_load[0])
    loads[place, 8:16, :] = jnp.where(left, nb_load[1], nb_load[2])
    for step in range(1, MATES):
        send(loads.at[place], loads.at[place], 2, mate(step))
    for f in range(4):
        y = jnp.transpose(ys[f])
        y = (y[:CASES] + y[CASES:]) * mask_pad[:, f * PAD : (f + 1) * PAD]
        own_y[f] = y
        send(own_y.at[f], nb_y.at[f ^ 1], 3, across[f])
    res = padded(res)
    for f in range(4):
        res_pad[f] = res[:, f * PAD : (f + 1) * PAD]

    col = iota((1, 256), 1)
    mode = col & 7
    tile = 2 * ((col >> 3) & 1) + (col >> 7)
    member = (col >> 4) & 7
    spare = (mode >= MODES) & (tile > 0)
    group = jnp.where(spare, 4, tile)
    mode = jnp.where(spare, 2 * (tile - 1) + mode - MODES, mode)
    d_sub = jnp.where(group == 1, -1, jnp.where(group == 2, 1, 0))
    d_grp = jnp.where(group == 3, -1, jnp.where(group == 4, 1, 0))
    source = ((member >> 2) + d_sub + 1) * 24 + ((member & 3) + d_grp) * MODES + mode
    source = jnp.where(mode < MODES, source, -1)
    pick = jnp.where(iota((128, 256), 0) == source, 1.0, 0.0).astype(BF16)

    slots_of = (
        place,
        core * g + (1 - core) * (8 + g),
        core * (12 + g) + (1 - core) * (4 + g),
        core * 4 + (g + 3) % 4,
        core * 4 + (g + 1) % 4,
    )
    lane = iota((32, 128), 1)
    line = iota((32, 128), 0)
    mode = 4 * (lane >> 6) + (lane & 3)
    slot = (lane >> 2) & 15
    gram = jnp.zeros((8, 128), F32)
    for f in range(4):
        r_high, r_low = split(own_rf[f])
        n_high, n_low = split(jnp.concatenate([own_rf[f], nb_rf[f]], axis=0))
        piece = mm(
            jnp.concatenate([r_high, r_low], axis=0), jnp.concatenate([n_high, n_low], axis=0), NT
        )
        piece_high, piece_low = split(piece[:8] + piece[8:])
        wanted = jnp.where((line & 8) == 0, slots_of[0], slots_of[1 + f])
        hot = ((line & 7) == mode) & (mode < MODES) & (slot == wanted)
        piece = mm(
            jnp.concatenate([piece_high, piece_low], axis=0),
            jnp.where(hot, 1.0, 0.0).astype(BF16),
            NN,
        )
        gram = gram + piece[:8] + piece[8:]
    grams[place] = gram
    for step in range(1, MATES):
        send(grams.at[place], grams.at[place], 4, mate(step))

    rows_in[pair] = rows_out[pair]
    wait_recv(rows_in.at[0 : PAIRS - 1], 1)
    high, low = split(rows_in[...].reshape(PAIRS * 8, 128))
    piece = mm(jnp.concatenate([high, low], axis=0), pick, NN).astype(BF16)
    piece = jnp.concatenate([piece[: PAIRS * 8], piece[PAIRS * 8 :]], axis=1)

    wait_recv(loads.at[0 : MATES - 1], 2)
    every = loads[...]
    total = doubled(jnp.sum(every[:, 0:8, :], axis=0))
    line = both_sides(every.reshape(MATES * 16, 128))
    part = summed(mm(piece, jnp.concatenate([line, line], axis=0), NN))
    part = part.reshape(PAIRS, 8, 128) + jnp.where(row >= MODES, total, 0.0)[None]
    parts[...] = jnp.where(left[None], part, pltpu.roll(part, 4, 1))[:, 0:4, :]
    for step in range(1, PAIRS):
        other, target = peer(step)
        send(parts.at[other], got.at[pair], 5, target)
    got[pair] = parts[pair]

    wait_recv(nb_y, 3)
    trace_res = jnp.zeros((8, 128), F32)
    trace_image = jnp.zeros((8, 128), F32)
    for f in range(4):
        image = own_y[f] + jnp.where(active_pad[:, f * PAD : (f + 1) * PAD], nb_y[f], 0.0)
        nb_y[f] = image
        r_high, r_low = split(own_rf[f])
        b_high, b_low = split(jnp.concatenate([res_pad[f], image], axis=0))
        piece = mm(
            jnp.concatenate([r_high, r_low], axis=0),
            jnp.concatenate(
                [b_high[:CASES], b_low[:CASES], b_high[CASES:], b_low[CASES:]], axis=0
            ),
            NT,
        )
        piece = piece[:8] + piece[8:]
        trace_res = trace_res + piece[:, :128]
        trace_image = trace_image + piece[:, 128:]
    trace_res = summed(trace_res)
    trace_image = summed(trace_image)
    wait_recv(grams.at[0 : MATES - 1], 4)
    high, low = split(grams[...].reshape(MATES * 8, 128))
    gram = jnp.concatenate([high, low], axis=1)

    wait_recv(got.at[0 : PAIRS - 1], 5)
    amp = doubled(unpacked(jnp.sum(got[...], axis=0)))
    rr_row = amp[6:7, :]
    step_row = rr_row / amp[7:8, :]
    step_size = column_of(step_row)
    square = jnp.zeros((CASES, 128), F32)
    for f in range(4):
        u = res_pad[f] - step_size * nb_y[f]
        res_pad[f] = u
        for k in range(0, PAD, 128):
            square = square + u[:, k : k + 128] * u[:, k : k + 128]
    u_row = row_of(0.5 * jnp.sum(square, axis=1, keepdims=True))
    scaled = jnp.where(row < MODES, step_row * amp, 0.0)
    cross = jnp.sum(scaled * (trace_res - step_row * trace_image), axis=0, keepdims=True)
    own = jnp.where(row == 6, doubled(u_row + 2.0 * cross), scaled)
    amps[place] = packed(own)
    slot = 12 - 4 * core + g
    for other in range(8):
        send(amps.at[place], amps.at[slot], 6, (2 * beside + other // 4, other % 4))
    for step in range(1, MATES):
        send(amps.at[place], amps.at[place], 6, mate(step))
    wait_recv(amps.at[0:15], 6)
    every = amps[...]
    line = both_sides(every.reshape(64, 128))
    image = summed(mm(gram, jnp.concatenate([line, line], axis=0), NN))
    mates = unpacked(every[0:MATES]).reshape(MATES * 8, 128)
    spare = (iota((MATES * 8, 128), 0) & 7) >= MODES
    norm = jnp.sum(jnp.where(spare, mates, mates * image), axis=0, keepdims=True)
    norms[pair] = norm
    for step in range(1, PAIRS):
        send(norms.at[pair], norms.at[pair], 7, peer(step)[1])

    spread = []
    for f in range(4):
        a_high, a_low = split(jnp.concatenate([own, unpacked(amps[slots_of[1 + f]])], axis=0))
        r_high, r_low = split(jnp.concatenate([own_rf[f], nb_rf[f]], axis=0))
        back = mm(
            jnp.concatenate([a_high, a_low, a_high, a_low], axis=0),
            jnp.concatenate([r_high, r_high, r_low, r_low], axis=0),
            TN,
        )
        spread.append((res_pad[f] + back[:CASES])[:, :FACE])
    next_v[...] = jnp.concatenate(spread, axis=1)
    next_copy = pltpu.make_async_copy(next_v, res_out, out_sem.at[0])
    next_copy.start()
    wait_recv(norms.at[0 : PAIRS - 1], 7)
    ratio = column_of(jnp.sum(norms[...], axis=0) / rr_row)
    coef_out[...] = jnp.where(iota((CASES, 128), 1) < 64, step_size, ratio)

    wait_send(own_rf, 0)
    wait_send(rows_in.at[0 : PAIRS - 1], 1)
    wait_send(loads.at[0 : MATES - 1], 2)
    wait_send(own_y, 3)
    wait_send(grams.at[0 : MATES - 1], 4)
    wait_send(parts.at[0 : PAIRS - 1], 5)
    wait_send(amps.at[0:15], 6)
    wait_send(norms.at[0 : PAIRS - 1], 7)
    next_copy.wait()


def update(
    lam_hbm,
    dir_hbm,
    res_hbm,
    coef_hbm,
    sizes_hbm,
    lam_out,
    res_out,
    dir_out,
    coef_v,
    sizes_ref,
    lam_v,
    res_v,
    dir_v,
    sem,
):
    ins = [
        pltpu.make_async_copy(src, dst, sem.at[k])
        for k, (src, dst) in enumerate(
            (
                (sizes_hbm, sizes_ref),
                (dir_hbm, dir_v),
                (lam_hbm, lam_v),
                (coef_hbm, coef_v),
                (res_hbm, res_v),
            )
        )
    ]
    for copy in ins:
        copy.start()
    outs = [
        pltpu.make_async_copy(src, dst, sem.at[5 + k])
        for k, (src, dst) in enumerate(((lam_v, lam_out), (res_v, res_out), (dir_v, dir_out)))
    ]
    ins[0].wait()
    flat = iota((1, WIDTH), 1)
    face = face_at(flat, FACE)
    limit = jnp.zeros_like(face)
    for f in range(4):
        limit = jnp.where(face == f, sizes_ref[0, 0, f], limit)
    active = (flat - face * FACE) < limit
    ins[1].wait()
    dirn = jnp.where(active, dir_v[...], 0.0)
    ins[2].wait()
    ins[3].wait()
    coef = coef_v[...]
    step_size = coef[:, 0:1]
    ratio = coef[:, 64:65]
    lam_v[...] = jnp.where(active, lam_v[...], 0.0) + step_size * dirn
    outs[0].start()
    ins[4].wait()
    outs[1].start()
    dir_v[...] = res_v[...] + ratio * dirn
    outs[2].start()
    for copy in outs:
        copy.wait()


def on_device(
    multipliers,
    residual,
    direction,
    dual_operator,
    rigid_trace,
    coarse_inverse,
    face_sizes,
    slot_order,
):
    field = jax.ShapeDtypeStruct((CASES, WIDTH), F32)
    hbm = pl.BlockSpec(memory_space=pltpu.HBM)
    vmem = pl.BlockSpec(memory_space=pltpu.VMEM)
    res_next, coef = pl.pallas_call(
        kernel,
        out_shape=(field, jax.ShapeDtypeStruct((CASES, 128), F32)),
        in_specs=[hbm] * 7,
        out_specs=[hbm, vmem],
        scratch_shapes=[
            pltpu.VMEM((CASES, WIDTH), F32),
            pltpu.VMEM((CASES, WIDTH), F32),
            pltpu.VMEM((CASES, WIDTH), F32),
            pltpu.VMEM((WIDTH, WIDTH), F32),
            pltpu.VMEM((MODES, 1, WIDTH), F32),
            pltpu.VMEM((MODES, COARSE), F32),
            pltpu.VMEM((1, 1, WIDTH), jnp.int32),
            pltpu.SMEM((1, 1, 4), jnp.int32),
            pltpu.VMEM((WIDE, WIDTH), BF16),
            pltpu.VMEM((WIDTH, 256), BF16),
            pltpu.VMEM((4, 8, PAD), F32),
            pltpu.VMEM((4, 8, PAD), F32),
            pltpu.VMEM((4, CASES, PAD), F32),
            pltpu.VMEM((4, CASES, PAD), F32),
            pltpu.VMEM((4, CASES, PAD), F32),
            pltpu.VMEM((PAIRS, 8, 128), F32),
            pltpu.VMEM((PAIRS, 8, 128), F32),
            pltpu.VMEM((MATES, 16, 128), F32),
            pltpu.VMEM((PAIRS, 4, 128), F32),
            pltpu.VMEM((PAIRS, 4, 128), F32),
            pltpu.VMEM((MATES, 8, 128), F32),
            pltpu.VMEM((16, 4, 128), F32),
            pltpu.VMEM((PAIRS, 1, 128), F32),
            pltpu.SemaphoreType.DMA((7,)),
            pltpu.SemaphoreType.DMA((1,)),
            pltpu.SemaphoreType.DMA((8,)),
            pltpu.SemaphoreType.DMA((8,)),
        ],
        compiler_params=pltpu.CompilerParams(
            collective_id=0, has_side_effects=True, vmem_limit_bytes=62 * 1024 * 1024
        ),
    )(
        residual.reshape(CASES, WIDTH),
        direction.reshape(CASES, WIDTH),
        dual_operator.reshape(WIDTH, WIDTH),
        rigid_trace.transpose(0, 2, 1, 3).reshape(MODES, 1, WIDTH),
        coarse_inverse,
        face_sizes,
        slot_order,
    )
    outs = pl.pallas_call(
        update,
        out_shape=(field, field, field),
        in_specs=[hbm] * 5,
        out_specs=[hbm, hbm, hbm],
        scratch_shapes=[
            pltpu.VMEM((CASES, 128), F32),
            pltpu.SMEM((1, 1, 4), jnp.int32),
            pltpu.VMEM((CASES, WIDTH), F32),
            pltpu.VMEM((CASES, WIDTH), F32),
            pltpu.VMEM((CASES, WIDTH), F32),
            pltpu.SemaphoreType.DMA((8,)),
        ],
        compiler_params=pltpu.CompilerParams(vmem_limit_bytes=62 * 1024 * 1024),
    )(
        multipliers.reshape(CASES, WIDTH),
        direction.reshape(CASES, WIDTH),
        res_next,
        coef,
        face_sizes,
    )
    return tuple(x[None, None] for x in outs)


def solution(mesh):
    wide = P("sub", "grp", None, None)
    return jax.shard_map(
        on_device,
        mesh=mesh,
        in_specs=(wide, wide, wide, wide, wide, P(("sub", "grp"), None), P("sub", "grp", None), P("sub", "grp", None)),
        out_specs=(wide, wide, wide),
        check_vma=False,
    )
```

```python
import functools

import jax
import jax.numpy as jnp
from jax import lax
from jax.experimental import pallas as pl
from jax.experimental.pallas import tpu as pltpu
from jax.sharding import PartitionSpec as P

MESH = pl.DeviceIdType.MESH
F32 = jnp.float32
BF16 = jnp.bfloat16
NN = (((1,), (0,)), ((), ()))
NT = (((1,), (1,)), ((), ()))
TN = (((0,), (0,)), ((), ()))

CASES = 64
WIDTH = 1200
FACE = 300
PAD = 384
ROWS = 304
WIDE = 4 * PAD
MODES = 6
COARSE = 1536
PAIRS = 32
MATES = 8
BARRIER_AT = 240
PEERS = sorted(
    ((dx, dz) for dx in range(4) for dz in range(8) if dx or dz),
    key=lambda step: -min(step[0], 4 - step[0]) - min(step[1], 8 - step[1]),
)


def split(x):
    high = x.astype(BF16)
    return high, (x - high.astype(F32)).astype(BF16)


def mm(a, b, dims):
    return lax.dot_general(a, b, dims, preferred_element_type=F32)


def iota(shape, dim):
    return lax.broadcasted_iota(jnp.int32, shape, dim)


def face_at(lane, step):
    one = jnp.int32(1)
    zero = jnp.int32(0)
    return (
        jnp.where(lane >= step, one, zero)
        + jnp.where(lane >= 2 * step, one, zero)
        + jnp.where(lane >= 3 * step, one, zero)
    )


def row_of(column):
    eye = iota((CASES, 128), 0) == iota((CASES, 128), 1)
    return jnp.sum(jnp.where(eye, column, 0.0), axis=0, keepdims=True)


def column_of(row):
    eye = iota((CASES, 128), 0) == iota((CASES, 128), 1)
    return jnp.sum(jnp.where(eye, row, 0.0), axis=1, keepdims=True)


def packed(tile):
    left = iota((8, 128), 1) < 64
    return jnp.where(left, tile, pltpu.roll(tile, 4, 0))[0:4]


def unpacked(half):
    return jnp.concatenate([half, pltpu.roll(half, 64, half.ndim - 1)], axis=half.ndim - 2)


def doubled(x):
    return jnp.where(iota(x.shape, 1) < 64, x, pltpu.roll(x, 64, 1))


def lanes_split(x):
    high = x.astype(BF16).astype(F32)
    return jnp.where(iota(x.shape, 1) < 64, high, x - high).astype(BF16)


def both_sides(x):
    other = pltpu.roll(x, 64, 1)
    left = iota(x.shape, 1) < 64
    return jnp.concatenate(
        [lanes_split(jnp.where(left, x, other)), lanes_split(jnp.where(left, other, x))], axis=0
    )


def summed(x):
    return x + pltpu.roll(x, 64, 1)


def kernel(
    res_hbm,
    dir_hbm,
    dual_hbm,
    trace_hbm,
    inv_hbm,
    sizes_hbm,
    order_hbm,
    res_out,
    coef_out,
    next_v,
    coef_v,
    res_v,
    dir_v,
    dual_v,
    trace_v,
    inv_v,
    order_ref,
    sizes_ref,
    perm,
    halves,
    own_rf,
    nb_rf,
    res_pad,
    own_y,
    nb_y,
    rows_out,
    rows_in,
    loads,
    parts,
    got,
    grams,
    amps,
    norms,
    in_sem,
    out_sem,
    send_sem,
    recv_sem,
):
    s = lax.axis_index("sub")
    g = lax.axis_index("grp")
    pair = s // 2
    core = s % 2
    place = core * 4 + g

    copies_in = {}
    for k, (name, src, dst) in enumerate(
        (
            ("sizes", sizes_hbm, sizes_ref),
            ("order", order_hbm, order_ref),
            ("trace", trace_hbm, trace_v),
            ("dir", dir_hbm, dir_v),
            ("inv", inv_hbm, inv_v),
            ("dual", dual_hbm, dual_v),
            ("res", res_hbm, res_v),
        )
    ):
        copies_in[name] = pltpu.make_async_copy(src, dst, in_sem.at[k])
        copies_in[name].start()

    rows_in[...] = jnp.zeros_like(rows_in)
    across = (
        ((s + 63) % 64, g),
        ((s + 1) % 64, g),
        (s, (g + 3) % 4),
        (s, (g + 1) % 4),
    )

    def mate(step):
        other = (place + step) % MATES
        return (pair * 2 + other // 4, other % 4)

    def peer(step):
        dx, dz = step
        other = (pair // 8 + dx) % 4 * 8 + (pair + dz) % 8
        return other, (other * 2 + core, g)

    beside = (pair + 2 * core - 1 + PAIRS) % PAIRS

    barrier = pltpu.get_barrier_semaphore()
    for step in PEERS:
        pl.semaphore_signal(barrier, inc=1, device_id=peer(step)[1], device_id_type=MESH)
    for other in range(4):
        for target in ((2 * pair + 63) % 64, other), ((2 * pair + 2) % 64, other):
            pl.semaphore_signal(barrier, inc=1, device_id=target, device_id_type=MESH)
    for step in range(1, MATES):
        pl.semaphore_signal(barrier, inc=1, device_id=mate(step), device_id_type=MESH)

    def send(src, dst, phase, target):
        pltpu.make_async_remote_copy(
            src_ref=src,
            dst_ref=dst,
            send_sem=send_sem.at[phase],
            recv_sem=recv_sem.at[phase],
            device_id=target,
            device_id_type=MESH,
        ).start()

    def wait_recv(ref, phase):
        pltpu.make_async_copy(ref, ref, recv_sem.at[phase]).wait()

    def wait_send(ref, phase):
        pltpu.make_async_copy(ref, ref, send_sem.at[phase]).wait()

    def greeted():
        pl.semaphore_wait(barrier, PAIRS - 1 + 8 + MATES - 1)
        for f in range(4):
            send(own_rf.at[f], nb_rf.at[f ^ 1], 0, across[f])
        for step in PEERS:
            other, target = peer(step)
            send(rows_out.at[other, 0:MODES], rows_in.at[pair, 0:MODES], 1, target)

    copies_in["sizes"].wait()
    copies_in["order"].wait()

    def limits(face):
        out = jnp.zeros_like(face)
        for f in range(4):
            out = jnp.where(face == f, sizes_ref[0, 0, f], out)
        return out

    lane = iota((1, WIDE), 1)
    face = face_at(lane, PAD)
    active_pad = (lane - face * PAD) < limits(face)
    sign_pad = jnp.where((face & 1) == 0, -1.0, 1.0)
    mask_pad = jnp.where(active_pad, sign_pad, 0.0)
    lane = iota((1, 4 * ROWS), 1)
    face = face_at(lane, ROWS)
    active_row = (lane - face * ROWS) < limits(face)
    mask_row = jnp.where(active_row, jnp.where((face & 1) == 0, -1.0, 1.0), 0.0)
    left = iota((8, 128), 1) < 64
    row = iota((8, 128), 0)

    order = order_ref[0]
    order = order + (ROWS - FACE) * face_at(order, FACE)
    line = lax.broadcasted_iota(jnp.int16, (ROWS, WIDTH), 0)
    ones = jnp.ones((ROWS, WIDTH), BF16)
    for f in range(4):
        hot = line == jnp.broadcast_to((order - f * ROWS).astype(jnp.int16), (ROWS, WIDTH))
        perm[f * ROWS : (f + 1) * ROWS, :] = jnp.where(hot, ones, jnp.zeros_like(ones))

    copies_in["trace"].wait()
    trace = jnp.concatenate([trace_v[...].reshape(MODES, WIDTH), jnp.zeros((2, WIDTH), F32)], axis=0)
    low = trace - trace.astype(BF16).astype(F32)
    got_rf = mm(jnp.concatenate([trace, low], axis=0).astype(BF16), perm[...], NT)
    got_rf = (got_rf[:8] + got_rf[8:]) * mask_row
    for f in range(4):
        cut = got_rf[:, f * ROWS : (f + 1) * ROWS]
        own_rf[f] = jnp.concatenate([cut, jnp.zeros((8, PAD - ROWS), F32)], axis=1)

    copies_in["inv"].wait()
    rows = jnp.concatenate([inv_v[...], jnp.zeros((2, COARSE), F32)], axis=0)
    rows = jnp.concatenate([jnp.zeros((8, 24), F32), rows, jnp.zeros((8, 104), F32)], axis=1)
    for p in range(PAIRS):
        rows_out[p] = rows[:, 48 * p : 48 * p + 128]

    def padded(x, width):
        gap = jnp.zeros((CASES, width - FACE), F32)
        spread = []
        for f in range(4):
            spread += [x[:, f * FACE : (f + 1) * FACE], gap]
        return jnp.concatenate(spread, axis=1)

    copies_in["dir"].wait()
    high, low = split(padded(dir_v[...], ROWS) * mask_row)
    slots = mm(jnp.concatenate([high, low], axis=0), perm[...], NN)
    slots = slots[:CASES] + slots[CASES:]

    high, low = split(slots)
    both = jnp.concatenate([high, low], axis=0)
    copies_in["dual"].wait()
    for k in range(0, WIDTH, 240):
        if k == BARRIER_AT:
            greeted()
        f_high, f_low = split(dual_v[k : k + 240, :])
        z_high, z_low = split(mm(f_high, both, NT) + mm(f_low, both, NT))
        halves[k : k + 240, 0:128] = z_high
        halves[k : k + 240, 128:256] = z_low

    ys = []
    for f in range(4):
        y = mm(perm[f * ROWS : (f + 1) * ROWS, :], halves[...], NN)
        ys.append(y[:, :128] + y[:, 128:])
    curvature = mm(both, halves[...], NN)
    curvature = curvature[:, :128] + curvature[:, 128:]
    curvature = curvature[:CASES] + curvature[CASES:]
    diagonal = (iota((CASES, 128), 1) & 63) == iota((CASES, 128), 0)
    curv_row = summed(jnp.sum(jnp.where(diagonal, curvature, 0.0), axis=0, keepdims=True))
    copies_in["res"].wait()
    flat = iota((1, WIDTH), 1)
    flat_face = face_at(flat, FACE)
    active = (flat - flat_face * FACE) < limits(flat_face)
    res = jnp.where(active, res_v[...], 0.0)
    rr_row = row_of(0.5 * jnp.sum(res * res, axis=1, keepdims=True))
    wait_recv(nb_rf, 0)
    own_load = jnp.zeros((8, 128), F32)
    nb_load = []
    for f in range(4):
        cut = slice(f * PAD, (f + 1) * PAD)
        nb_rf[f] = jnp.where(active_pad[:, cut], nb_rf[f], 0.0)
        r_high, r_low = split(jnp.concatenate([own_rf[f, :, :ROWS], nb_rf[f, :, :ROWS]], axis=0))
        y_high, y_low = split(ys[f])
        piece = mm(
            jnp.concatenate([r_high, r_low], axis=0), jnp.concatenate([y_high, y_low], axis=1), NN
        )
        piece = piece[:, :128] + piece[:, 128:]
        piece = piece[:16] + piece[16:32]
        if not f & 1:
            piece = -piece
        own_load = own_load + piece[:8]
        nb_load.append(summed(piece[8:]))
    own_load = summed(own_load)
    own_load = jnp.where(row == 6, rr_row, jnp.where(row == 7, curv_row, own_load))
    for f in range(3):
        moved = pltpu.roll(nb_load[3], 6 - 2 * f, 0)
        nb_load[f] = jnp.where(row < MODES, nb_load[f], moved)
    loads[place, 0:8, :] = jnp.where(left, own_load, nb_load[0])
    loads[place, 8:16, :] = jnp.where(left, nb_load[1], nb_load[2])
    for step in range(1, MATES):
        send(loads.at[place], loads.at[place], 2, mate(step))
    for f in range(4):
        y = jnp.transpose(jnp.concatenate([ys[f], jnp.zeros((PAD - ROWS, 128), F32)], axis=0))
        y = (y[:CASES] + y[CASES:]) * mask_pad[:, f * PAD : (f + 1) * PAD]
        own_y[f] = y
        send(own_y.at[f], nb_y.at[f ^ 1], 3, across[f])
    res = padded(res, PAD)
    for f in range(4):
        res_pad[f] = res[:, f * PAD : (f + 1) * PAD]

    col = iota((1, 256), 1)
    mode = col & 7
    tile = 2 * ((col >> 3) & 1) + (col >> 7)
    member = (col >> 4) & 7
    spare = (mode >= MODES) & (tile > 0)
    group = jnp.where(spare, 4, tile)
    mode = jnp.where(spare, 2 * (tile - 1) + mode - MODES, mode)
    d_sub = jnp.where(group == 1, -1, jnp.where(group == 2, 1, 0))
    d_grp = jnp.where(group == 3, -1, jnp.where(group == 4, 1, 0))
    source = ((member >> 2) + d_sub + 1) * 24 + ((member & 3) + d_grp) * MODES + mode
    source = jnp.where(mode < MODES, source, -1)
    pick = jnp.where(iota((128, 256), 0) == source, 1.0, 0.0).astype(BF16)

    slots_of = (
        place,
        core * g + (1 - core) * (8 + g),
        core * (12 + g) + (1 - core) * (4 + g),
        core * 4 + (g + 3) % 4,
        core * 4 + (g + 1) % 4,
    )
    lane = iota((32, 128), 1)
    line = iota((32, 128), 0)
    mode = 4 * (lane >> 6) + (lane & 3)
    slot = (lane >> 2) & 15
    gram = jnp.zeros((8, 128), F32)
    for f in range(4):
        r_high, r_low = split(own_rf[f])
        n_high, n_low = split(jnp.concatenate([own_rf[f], nb_rf[f]], axis=0))
        piece = mm(
            jnp.concatenate([r_high, r_low], axis=0), jnp.concatenate([n_high, n_low], axis=0), NT
        )
        piece_high, piece_low = split(piece[:8] + piece[8:])
        wanted = jnp.where((line & 8) == 0, slots_of[0], slots_of[1 + f])
        hot = ((line & 7) == mode) & (mode < MODES) & (slot == wanted)
        piece = mm(
            jnp.concatenate([piece_high, piece_low], axis=0),
            jnp.where(hot, 1.0, 0.0).astype(BF16),
            NN,
        )
        gram = gram + piece[:8] + piece[8:]
    grams[place] = gram

    rows_in[pair] = rows_out[pair]
    wait_recv(rows_in.at[0 : PAIRS - 1, 0:MODES], 1)
    high, low = split(rows_in[...].reshape(PAIRS * 8, 128))
    piece = mm(jnp.concatenate([high, low], axis=0), pick, NN).astype(BF16)
    piece = jnp.concatenate([piece[: PAIRS * 8], piece[PAIRS * 8 :]], axis=1)

    for step in range(1, MATES):
        send(grams.at[place], grams.at[place], 4, mate(step))

    wait_recv(loads.at[0 : MATES - 1], 2)
    every = loads[...]
    total = doubled(jnp.sum(every[:, 0:8, :], axis=0))
    line = both_sides(every.reshape(MATES * 16, 128))
    part = summed(mm(piece, jnp.concatenate([line, line], axis=0), NN))
    part = part.reshape(PAIRS, 8, 128) + jnp.where(row >= MODES, total, 0.0)[None]
    parts[...] = jnp.where(left[None], part, pltpu.roll(part, 4, 1))[:, 0:4, :]
    for step in PEERS:
        other, target = peer(step)
        send(parts.at[other], got.at[pair], 5, target)
    got[pair] = parts[pair]

    wait_recv(nb_y, 3)
    trace_res = jnp.zeros((8, 128), F32)
    trace_image = jnp.zeros((8, 128), F32)
    for f in range(4):
        image = own_y[f] + jnp.where(active_pad[:, f * PAD : (f + 1) * PAD], nb_y[f], 0.0)
        nb_y[f] = image
        r_high, r_low = split(own_rf[f])
        b_high, b_low = split(jnp.concatenate([res_pad[f], image], axis=0))
        piece = mm(
            jnp.concatenate([r_high, r_low], axis=0),
            jnp.concatenate(
                [b_high[:CASES], b_low[:CASES], b_high[CASES:], b_low[CASES:]], axis=0
            ),
            NT,
        )
        piece = piece[:8] + piece[8:]
        trace_res = trace_res + piece[:, :128]
        trace_image = trace_image + piece[:, 128:]
    trace_res = summed(trace_res)
    trace_image = summed(trace_image)
    wait_recv(grams.at[0 : MATES - 1], 4)
    high, low = split(grams[...].reshape(MATES * 8, 128))
    gram = jnp.concatenate([high, low], axis=1)

    wait_recv(got.at[0 : PAIRS - 1], 5)
    amp = doubled(unpacked(jnp.sum(got[...], axis=0)))
    rr_row = amp[6:7, :]
    step_row = rr_row / amp[7:8, :]
    step_size = column_of(step_row)
    square = jnp.zeros((CASES, 128), F32)
    for f in range(4):
        u = res_pad[f] - step_size * nb_y[f]
        res_pad[f] = u
        for k in range(0, PAD, 128):
            square = square + u[:, k : k + 128] * u[:, k : k + 128]
    u_row = row_of(0.5 * jnp.sum(square, axis=1, keepdims=True))
    scaled = jnp.where(row < MODES, step_row * amp, 0.0)
    cross = jnp.sum(scaled * (trace_res - step_row * trace_image), axis=0, keepdims=True)
    own = jnp.where(row == 6, doubled(u_row + 2.0 * cross), scaled)
    amps[place] = packed(own)
    slot = 12 - 4 * core + g
    for other in range(8):
        send(amps.at[place], amps.at[slot], 6, (2 * beside + other // 4, other % 4))
    for step in range(1, MATES):
        send(amps.at[place], amps.at[place], 6, mate(step))
    wait_recv(amps.at[0:15], 6)
    every = amps[...]
    line = both_sides(every.reshape(64, 128))
    image = summed(mm(gram, jnp.concatenate([line, line], axis=0), NN))
    mates = unpacked(every[0:MATES]).reshape(MATES * 8, 128)
    spare = (iota((MATES * 8, 128), 0) & 7) >= MODES
    norm = jnp.sum(jnp.where(spare, mates, mates * image), axis=0, keepdims=True)
    norms[pair] = norm
    for step in PEERS:
        send(norms.at[pair], norms.at[pair], 7, peer(step)[1])

    spread = []
    for f in range(4):
        a_high, a_low = split(jnp.concatenate([own, unpacked(amps[slots_of[1 + f]])], axis=0))
        r_high, r_low = split(jnp.concatenate([own_rf[f], nb_rf[f]], axis=0))
        back = mm(
            jnp.concatenate([a_high, a_low, a_high, a_low], axis=0),
            jnp.concatenate([r_high, r_high, r_low, r_low], axis=0),
            TN,
        )
        spread.append((res_pad[f] + back[:CASES])[:, :FACE])
    next_v[...] = jnp.concatenate(spread, axis=1)
    next_copy = pltpu.make_async_copy(next_v, res_out, out_sem.at[0])
    next_copy.start()
    wait_recv(norms.at[0 : PAIRS - 1], 7)
    ratio = jnp.sum(norms[...], axis=0) / rr_row
    coef_v[...] = jnp.where(row == 0, step_row, ratio)
    coef_copy = pltpu.make_async_copy(coef_v, coef_out, out_sem.at[1])
    coef_copy.start()

    wait_send(own_rf, 0)
    wait_send(rows_in.at[0 : PAIRS - 1, 0:MODES], 1)
    wait_send(loads.at[0 : MATES - 1], 2)
    wait_send(own_y, 3)
    wait_send(grams.at[0 : MATES - 1], 4)
    wait_send(parts.at[0 : PAIRS - 1], 5)
    wait_send(amps.at[0:15], 6)
    wait_send(norms.at[0 : PAIRS - 1], 7)
    next_copy.wait()
    coef_copy.wait()


def update(
    lam_hbm,
    dir_hbm,
    res_hbm,
    coef_hbm,
    sizes_hbm,
    lam_out,
    res_out,
    dir_out,
    coef_v,
    sizes_ref,
    lam_v,
    res_v,
    dir_v,
    sem,
):
    first = [
        pltpu.make_async_copy(sizes_hbm, sizes_ref, sem.at[0]),
        pltpu.make_async_copy(coef_hbm, coef_v, sem.at[1]),
    ]
    ins = [
        pltpu.make_async_copy(src, dst, sem.at[2 + k])
        for k, (src, dst) in enumerate(((dir_hbm, dir_v), (lam_hbm, lam_v), (res_hbm, res_v)))
    ]
    outs = [
        pltpu.make_async_copy(src, dst, sem.at[5 + k])
        for k, (src, dst) in enumerate(((lam_v, lam_out), (res_v, res_out), (dir_v, dir_out)))
    ]
    for one in first + ins:
        one.start()
    first[0].wait()
    flat = iota((1, WIDTH), 1)
    face = face_at(flat, FACE)
    limit = jnp.zeros_like(face)
    for f in range(4):
        limit = jnp.where(face == f, sizes_ref[0, 0, f], limit)
    active = (flat - face * FACE) < limit
    first[1].wait()
    step_size = column_of(coef_v[0:1, :])
    ratio = column_of(coef_v[1:2, :])
    for one in ins[0:2]:
        one.wait()
    dirn = jnp.where(active, dir_v[...], 0.0)
    lam_v[...] = jnp.where(active, lam_v[...], 0.0) + step_size * dirn
    outs[0].start()
    ins[2].wait()
    outs[1].start()
    dir_v[...] = res_v[...] + ratio * dirn
    outs[2].start()
    for one in outs:
        one.wait()


def on_device(
    multipliers,
    residual,
    direction,
    dual_operator,
    rigid_trace,
    coarse_inverse,
    face_sizes,
    slot_order,
):
    field = jax.ShapeDtypeStruct((CASES, WIDTH), F32)
    hbm = pl.BlockSpec(memory_space=pltpu.HBM)
    res_next, coef = pl.pallas_call(
        kernel,
        out_shape=(field, jax.ShapeDtypeStruct((8, 128), F32)),
        in_specs=[hbm] * 7,
        out_specs=[hbm, hbm],
        scratch_shapes=[
            pltpu.VMEM((CASES, WIDTH), F32),
            pltpu.VMEM((8, 128), F32),
            pltpu.VMEM((CASES, WIDTH), F32),
            pltpu.VMEM((CASES, WIDTH), F32),
            pltpu.VMEM((WIDTH, WIDTH), F32),
            pltpu.VMEM((MODES, 1, WIDTH), F32),
            pltpu.VMEM((MODES, COARSE), F32),
            pltpu.VMEM((1, 1, WIDTH), jnp.int32),
            pltpu.SMEM((1, 1, 4), jnp.int32),
            pltpu.VMEM((4 * ROWS, WIDTH), BF16),
            pltpu.VMEM((WIDTH, 256), BF16),
            pltpu.VMEM((4, 8, PAD), F32),
            pltpu.VMEM((4, 8, PAD), F32),
            pltpu.VMEM((4, CASES, PAD), F32),
            pltpu.VMEM((4, CASES, PAD), F32),
            pltpu.VMEM((4, CASES, PAD), F32),
            pltpu.VMEM((PAIRS, 8, 128), F32),
            pltpu.VMEM((PAIRS, 8, 128), F32),
            pltpu.VMEM((MATES, 16, 128), F32),
            pltpu.VMEM((PAIRS, 4, 128), F32),
            pltpu.VMEM((PAIRS, 4, 128), F32),
            pltpu.VMEM((MATES, 8, 128), F32),
            pltpu.VMEM((16, 4, 128), F32),
            pltpu.VMEM((PAIRS, 1, 128), F32),
            pltpu.SemaphoreType.DMA((7,)),
            pltpu.SemaphoreType.DMA((2,)),
            pltpu.SemaphoreType.DMA((8,)),
            pltpu.SemaphoreType.DMA((8,)),
        ],
        compiler_params=pltpu.CompilerParams(
            collective_id=0, has_side_effects=True, vmem_limit_bytes=62 * 1024 * 1024
        ),
    )(
        residual.reshape(CASES, WIDTH),
        direction.reshape(CASES, WIDTH),
        dual_operator.reshape(WIDTH, WIDTH),
        rigid_trace.transpose(0, 2, 1, 3).reshape(MODES, 1, WIDTH),
        coarse_inverse,
        face_sizes,
        slot_order,
    )
    outs = pl.pallas_call(
        update,
        out_shape=(field, field, field),
        in_specs=[hbm] * 5,
        out_specs=[hbm, hbm, hbm],
        scratch_shapes=[
            pltpu.VMEM((8, 128), F32),
            pltpu.SMEM((1, 1, 4), jnp.int32),
            pltpu.VMEM((CASES, WIDTH), F32),
            pltpu.VMEM((CASES, WIDTH), F32),
            pltpu.VMEM((CASES, WIDTH), F32),
            pltpu.SemaphoreType.DMA((8,)),
        ],
        compiler_params=pltpu.CompilerParams(vmem_limit_bytes=62 * 1024 * 1024),
    )(
        multipliers.reshape(CASES, WIDTH),
        direction.reshape(CASES, WIDTH),
        res_next,
        coef,
        face_sizes,
    )
    return tuple(x[None, None] for x in outs)


def solution(mesh):
    wide = P("sub", "grp", None, None)
    return jax.shard_map(
        on_device,
        mesh=mesh,
        in_specs=(wide, wide, wide, wide, wide, P(("sub", "grp"), None), P("sub", "grp", None), P("sub", "grp", None)),
        out_specs=(wide, wide, wide),
        check_vma=False,
    )
```

```python
import functools

import jax
import jax.numpy as jnp
from jax import lax
from jax.experimental import pallas as pl
from jax.experimental.pallas import tpu as pltpu
from jax.sharding import PartitionSpec as P

MESH = pl.DeviceIdType.MESH
F32 = jnp.float32
BF16 = jnp.bfloat16
NN = (((1,), (0,)), ((), ()))
NT = (((1,), (1,)), ((), ()))
TN = (((0,), (0,)), ((), ()))

CASES = 64
WIDTH = 1200
FACE = 300
PAD = 384
ROWS = 304
WIDE = 4 * PAD
MODES = 6
COARSE = 1536
PAIRS = 32
MATES = 8
BARRIER_AT = 240
PEERS = sorted(
    ((dx, dz) for dx in range(4) for dz in range(8) if dx or dz),
    key=lambda step: -min(step[0], 4 - step[0]) - min(step[1], 8 - step[1]),
)


def split(x):
    high = x.astype(BF16)
    return high, (x - high.astype(F32)).astype(BF16)


def mm(a, b, dims):
    return lax.dot_general(a, b, dims, preferred_element_type=F32)


def iota(shape, dim):
    return lax.broadcasted_iota(jnp.int32, shape, dim)


def face_at(lane, step):
    one = jnp.int32(1)
    zero = jnp.int32(0)
    return (
        jnp.where(lane >= step, one, zero)
        + jnp.where(lane >= 2 * step, one, zero)
        + jnp.where(lane >= 3 * step, one, zero)
    )


def row_of(column):
    eye = iota((CASES, 128), 0) == iota((CASES, 128), 1)
    return jnp.sum(jnp.where(eye, column, 0.0), axis=0, keepdims=True)


def column_of(row):
    eye = iota((CASES, 128), 0) == iota((CASES, 128), 1)
    return jnp.sum(jnp.where(eye, row, 0.0), axis=1, keepdims=True)


def packed(tile):
    left = iota((8, 128), 1) < 64
    return jnp.where(left, tile, pltpu.roll(tile, 4, 0))[0:4]


def unpacked(half):
    return jnp.concatenate([half, pltpu.roll(half, 64, half.ndim - 1)], axis=half.ndim - 2)


def doubled(x):
    return jnp.where(iota(x.shape, 1) < 64, x, pltpu.roll(x, 64, 1))


def lanes_split(x):
    high = x.astype(BF16).astype(F32)
    return jnp.where(iota(x.shape, 1) < 64, high, x - high).astype(BF16)


def both_sides(x):
    other = pltpu.roll(x, 64, 1)
    left = iota(x.shape, 1) < 64
    return jnp.concatenate(
        [lanes_split(jnp.where(left, x, other)), lanes_split(jnp.where(left, other, x))], axis=0
    )


def summed(x):
    return x + pltpu.roll(x, 64, 1)


def kernel(
    res_hbm,
    dir_hbm,
    dual_hbm,
    trace_hbm,
    inv_hbm,
    sizes_hbm,
    order_hbm,
    res_out,
    coef_out,
    next_v,
    coef_v,
    res_v,
    dir_v,
    dual_v,
    trace_v,
    inv_v,
    order_ref,
    sizes_ref,
    perm,
    halves,
    own_rf,
    nb_rf,
    res_pad,
    own_y,
    nb_y,
    rows_out,
    rows_in,
    loads,
    parts,
    got,
    got_next,
    grams,
    amps,
    amp_before,
    norms,
    in_sem,
    out_sem,
    send_sem,
    recv_sem,
):
    s = lax.axis_index("sub")
    g = lax.axis_index("grp")
    pair = s // 2
    core = s % 2
    place = core * 4 + g

    copies_in = {}
    for k, (name, src, dst) in enumerate(
        (
            ("sizes", sizes_hbm, sizes_ref),
            ("order", order_hbm, order_ref),
            ("trace", trace_hbm, trace_v),
            ("dir", dir_hbm, dir_v),
            ("inv", inv_hbm, inv_v),
            ("dual", dual_hbm, dual_v),
            ("res", res_hbm, res_v),
        )
    ):
        copies_in[name] = pltpu.make_async_copy(src, dst, in_sem.at[k])
        copies_in[name].start()

    rows_in[...] = jnp.zeros_like(rows_in)
    across = (
        ((s + 63) % 64, g),
        ((s + 1) % 64, g),
        (s, (g + 3) % 4),
        (s, (g + 1) % 4),
    )

    def mate(step):
        other = (place + step) % MATES
        return (pair * 2 + other // 4, other % 4)

    def peer(step):
        dx, dz = step
        other = (pair // 8 + dx) % 4 * 8 + (pair + dz) % 8
        return other, (other * 2 + core, g)

    has_next = (core == 1) & (pair < PAIRS - 1)
    has_before = (core == 0) & (pair > 0)

    barrier = pltpu.get_barrier_semaphore()
    for step in PEERS:
        pl.semaphore_signal(barrier, inc=1, device_id=peer(step)[1], device_id_type=MESH)
    pl.semaphore_signal(
        barrier, inc=1, device_id=((s + 2 * core + 63) % 64, g), device_id_type=MESH
    )

    @pl.when(core == 1)
    def _():
        for step in PEERS:
            other = peer(step)[0]
            pl.semaphore_signal(barrier, inc=1, device_id=(2 * other, g), device_id_type=MESH)

    for step in range(1, MATES):
        pl.semaphore_signal(barrier, inc=1, device_id=mate(step), device_id_type=MESH)

    def send(src, dst, phase, target):
        pltpu.make_async_remote_copy(
            src_ref=src,
            dst_ref=dst,
            send_sem=send_sem.at[phase],
            recv_sem=recv_sem.at[phase],
            device_id=target,
            device_id_type=MESH,
        ).start()

    def wait_recv(ref, phase):
        pltpu.make_async_copy(ref, ref, recv_sem.at[phase]).wait()

    def wait_send(ref, phase):
        pltpu.make_async_copy(ref, ref, send_sem.at[phase]).wait()

    def greeted():
        pl.semaphore_wait(barrier, (PAIRS - 1) * (2 - core) + 1 + MATES - 1)
        for f in range(4):
            send(own_rf.at[f], nb_rf.at[f ^ 1], 0, across[f])
        for step in PEERS:
            other, target = peer(step)
            send(rows_out.at[other, 0:MODES], rows_in.at[pair, 0:MODES], 1, target)

    copies_in["sizes"].wait()
    copies_in["order"].wait()

    def limits(face):
        out = jnp.zeros_like(face)
        for f in range(4):
            out = jnp.where(face == f, sizes_ref[0, 0, f], out)
        return out

    lane = iota((1, WIDE), 1)
    face = face_at(lane, PAD)
    active_pad = (lane - face * PAD) < limits(face)
    sign_pad = jnp.where((face & 1) == 0, -1.0, 1.0)
    mask_pad = jnp.where(active_pad, sign_pad, 0.0)
    lane = iota((1, 4 * ROWS), 1)
    face = face_at(lane, ROWS)
    active_row = (lane - face * ROWS) < limits(face)
    mask_row = jnp.where(active_row, jnp.where((face & 1) == 0, -1.0, 1.0), 0.0)
    left = iota((8, 128), 1) < 64
    row = iota((8, 128), 0)

    order = order_ref[0]
    order = order + (ROWS - FACE) * face_at(order, FACE)
    line = lax.broadcasted_iota(jnp.int16, (ROWS, WIDTH), 0)
    ones = jnp.ones((ROWS, WIDTH), BF16)
    for f in range(4):
        hot = line == jnp.broadcast_to((order - f * ROWS).astype(jnp.int16), (ROWS, WIDTH))
        perm[f * ROWS : (f + 1) * ROWS, :] = jnp.where(hot, ones, jnp.zeros_like(ones))

    copies_in["trace"].wait()
    trace = jnp.concatenate([trace_v[...].reshape(MODES, WIDTH), jnp.zeros((2, WIDTH), F32)], axis=0)
    low = trace - trace.astype(BF16).astype(F32)
    got_rf = mm(jnp.concatenate([trace, low], axis=0).astype(BF16), perm[...], NT)
    got_rf = (got_rf[:8] + got_rf[8:]) * mask_row
    for f in range(4):
        cut = got_rf[:, f * ROWS : (f + 1) * ROWS]
        own_rf[f] = jnp.concatenate([cut, jnp.zeros((8, PAD - ROWS), F32)], axis=1)

    copies_in["inv"].wait()
    rows = jnp.concatenate([inv_v[...], jnp.zeros((2, COARSE), F32)], axis=0)
    rows = jnp.concatenate([jnp.zeros((8, 24), F32), rows, jnp.zeros((8, 104), F32)], axis=1)
    for p in range(PAIRS):
        rows_out[p] = rows[:, 48 * p : 48 * p + 128]

    def padded(x, width):
        gap = jnp.zeros((CASES, width - FACE), F32)
        spread = []
        for f in range(4):
            spread += [x[:, f * FACE : (f + 1) * FACE], gap]
        return jnp.concatenate(spread, axis=1)

    copies_in["dir"].wait()
    high, low = split(padded(dir_v[...], ROWS) * mask_row)
    slots = mm(jnp.concatenate([high, low], axis=0), perm[...], NN)
    slots = slots[:CASES] + slots[CASES:]

    high, low = split(slots)
    both = jnp.concatenate([high, low], axis=0)
    copies_in["dual"].wait()
    for k in range(0, WIDTH, 240):
        if k == BARRIER_AT:
            greeted()
        f_high, f_low = split(dual_v[k : k + 240, :])
        z_high, z_low = split(mm(f_high, both, NT) + mm(f_low, both, NT))
        halves[k : k + 240, 0:128] = z_high
        halves[k : k + 240, 128:256] = z_low

    ys = []
    for f in range(4):
        y = mm(perm[f * ROWS : (f + 1) * ROWS, :], halves[...], NN)
        ys.append(y[:, :128] + y[:, 128:])
    curvature = mm(both, halves[...], NN)
    curvature = curvature[:, :128] + curvature[:, 128:]
    curvature = curvature[:CASES] + curvature[CASES:]
    diagonal = (iota((CASES, 128), 1) & 63) == iota((CASES, 128), 0)
    curv_row = summed(jnp.sum(jnp.where(diagonal, curvature, 0.0), axis=0, keepdims=True))
    copies_in["res"].wait()
    flat = iota((1, WIDTH), 1)
    flat_face = face_at(flat, FACE)
    active = (flat - flat_face * FACE) < limits(flat_face)
    res = jnp.where(active, res_v[...], 0.0)
    rr_row = row_of(0.5 * jnp.sum(res * res, axis=1, keepdims=True))
    wait_recv(nb_rf, 0)
    own_load = jnp.zeros((8, 128), F32)
    nb_load = []
    for f in range(4):
        cut = slice(f * PAD, (f + 1) * PAD)
        nb_rf[f] = jnp.where(active_pad[:, cut], nb_rf[f], 0.0)
        r_high, r_low = split(jnp.concatenate([own_rf[f, :, :ROWS], nb_rf[f, :, :ROWS]], axis=0))
        y_high, y_low = split(ys[f])
        piece = mm(
            jnp.concatenate([r_high, r_low], axis=0), jnp.concatenate([y_high, y_low], axis=1), NN
        )
        piece = piece[:, :128] + piece[:, 128:]
        piece = piece[:16] + piece[16:32]
        if not f & 1:
            piece = -piece
        own_load = own_load + piece[:8]
        nb_load.append(summed(piece[8:]))
    own_load = summed(own_load)
    own_load = jnp.where(row == 6, rr_row, jnp.where(row == 7, curv_row, own_load))
    for f in range(3):
        moved = pltpu.roll(nb_load[3], 6 - 2 * f, 0)
        nb_load[f] = jnp.where(row < MODES, nb_load[f], moved)
    loads[place, 0:8, :] = jnp.where(left, own_load, nb_load[0])
    loads[place, 8:16, :] = jnp.where(left, nb_load[1], nb_load[2])
    for step in range(1, MATES):
        send(loads.at[place], loads.at[place], 2, mate(step))
    for f in range(4):
        y = jnp.transpose(jnp.concatenate([ys[f], jnp.zeros((PAD - ROWS, 128), F32)], axis=0))
        y = (y[:CASES] + y[CASES:]) * mask_pad[:, f * PAD : (f + 1) * PAD]
        own_y[f] = y
        send(own_y.at[f], nb_y.at[f ^ 1], 3, across[f])
    res = padded(res, PAD)
    for f in range(4):
        res_pad[f] = res[:, f * PAD : (f + 1) * PAD]

    col = iota((1, 256), 1)
    mode = col & 7
    tile = 2 * ((col >> 3) & 1) + (col >> 7)
    member = (col >> 4) & 7
    spare = (mode >= MODES) & (tile > 0)
    group = jnp.where(spare, 4, tile)
    mode = jnp.where(spare, 2 * (tile - 1) + mode - MODES, mode)
    d_sub = jnp.where(group == 1, -1, jnp.where(group == 2, 1, 0))
    d_grp = jnp.where(group == 3, -1, jnp.where(group == 4, 1, 0))
    source = ((member >> 2) + d_sub + 1) * 24 + ((member & 3) + d_grp) * MODES + mode
    source = jnp.where(mode < MODES, source, -1)
    pick = jnp.where(iota((128, 256), 0) == source, 1.0, 0.0).astype(BF16)

    slots_of = (
        place,
        core * g + (1 - core) * MATES,
        core * MATES + (1 - core) * (4 + g),
        core * 4 + (g + 3) % 4,
        core * 4 + (g + 1) % 4,
    )
    lane = iota((32, 128), 1)
    line = iota((32, 128), 0)
    mode = 4 * (lane >> 5) + (lane & 3)
    slot = (lane >> 2) & 7
    gram = jnp.zeros((8, 128), F32)
    for f in range(4):
        r_high, r_low = split(own_rf[f])
        n_high, n_low = split(jnp.concatenate([own_rf[f], nb_rf[f]], axis=0))
        piece = mm(
            jnp.concatenate([r_high, r_low], axis=0), jnp.concatenate([n_high, n_low], axis=0), NT
        )
        piece = piece[:8] + piece[8:]
        if f == 1:
            edge = piece[:, 8:16]
        piece_high, piece_low = split(piece)
        wanted = jnp.where((line & 8) == 0, slots_of[0], slots_of[1 + f])
        hot = ((line & 7) == mode) & (mode < MODES) & (slot == wanted)
        piece = mm(
            jnp.concatenate([piece_high, piece_low], axis=0),
            jnp.where(hot, 1.0, 0.0).astype(BF16),
            NN,
        )
        gram = gram + piece[:8] + piece[8:]
    grams[place] = gram

    rows_in[pair] = rows_out[pair]
    wait_recv(rows_in.at[0 : PAIRS - 1, 0:MODES], 1)
    high, low = split(rows_in[...].reshape(PAIRS * 8, 128))
    piece = mm(jnp.concatenate([high, low], axis=0), pick, NN).astype(BF16)
    piece = jnp.concatenate([piece[: PAIRS * 8], piece[PAIRS * 8 :]], axis=1)

    for step in range(1, MATES):
        send(grams.at[place], grams.at[place], 4, mate(step))

    wait_recv(loads.at[0 : MATES - 1], 2)
    every = loads[...]
    total = doubled(jnp.sum(every[:, 0:8, :], axis=0))
    line = both_sides(every.reshape(MATES * 16, 128))
    part = summed(mm(piece, jnp.concatenate([line, line], axis=0), NN))
    part = part.reshape(PAIRS, 8, 128) + jnp.where(row >= MODES, total, 0.0)[None]
    parts[...] = jnp.where(left[None], part, pltpu.roll(part, 4, 1))[:, 0:4, :]
    @pl.when(core == 0)
    def _():
        for step in PEERS:
            other, target = peer(step)
            send(parts.at[other], got_next.at[pair], 8, ((2 * other + 63) % 64, g))
            send(parts.at[other], got.at[pair], 5, target)
        send(parts.at[pair], got_next.at[pair], 8, ((2 * pair + 63) % 64, g))

    @pl.when(core == 1)
    def _():
        for step in PEERS:
            other, target = peer(step)
            send(parts.at[other], got.at[pair], 5, target)

    got[pair] = parts[pair]

    wait_recv(nb_y, 3)
    trace_res = jnp.zeros((8, 128), F32)
    trace_image = jnp.zeros((8, 128), F32)
    for f in range(4):
        image = own_y[f] + jnp.where(active_pad[:, f * PAD : (f + 1) * PAD], nb_y[f], 0.0)
        nb_y[f] = image
        r_high, r_low = split(own_rf[f])
        b_high, b_low = split(jnp.concatenate([res_pad[f], image], axis=0))
        piece = mm(
            jnp.concatenate([r_high, r_low], axis=0),
            jnp.concatenate(
                [b_high[:CASES], b_low[:CASES], b_high[CASES:], b_low[CASES:]], axis=0
            ),
            NT,
        )
        piece = piece[:8] + piece[8:]
        trace_res = trace_res + piece[:, :128]
        trace_image = trace_image + piece[:, 128:]
    trace_res = summed(trace_res)
    trace_image = summed(trace_image)
    wait_recv(grams.at[0 : MATES - 1], 4)
    gram = lanes_split(summed(grams[...].reshape(MATES * 8, 128)))

    wait_recv(got.at[0 : PAIRS - 1], 5)
    pl.when(core == 1)(lambda: wait_recv(got_next, 8))
    amp = doubled(unpacked(jnp.sum(got[...], axis=0)))
    rr_row = amp[6:7, :]
    step_row = rr_row / amp[7:8, :]
    step_size = column_of(step_row)
    square = jnp.zeros((CASES, 128), F32)
    for f in range(4):
        u = res_pad[f] - step_size * nb_y[f]
        res_pad[f] = u
        for k in range(0, PAD, 128):
            square = square + u[:, k : k + 128] * u[:, k : k + 128]
    u_row = row_of(0.5 * jnp.sum(square, axis=1, keepdims=True))
    scaled = jnp.where(row < MODES, step_row * amp, 0.0)
    after = doubled(unpacked(jnp.sum(got_next[...], axis=0)))
    after = jnp.where((row < MODES) & has_next, step_row * after, 0.0)
    cross = trace_res - step_row * trace_image
    for k in range(MODES):
        cross = cross + edge[:, k : k + 1] * after[k : k + 1, :]
    cross = jnp.sum(scaled * cross, axis=0, keepdims=True)
    own = jnp.where(row == 6, doubled(u_row + 2.0 * cross), scaled)
    amps[place] = packed(own)
    for step in range(1, MATES):
        send(amps.at[place], amps.at[place], 6, mate(step))

    @pl.when(has_next)
    def _():
        send(amps.at[place], amp_before, 9, (2 * pair + 2, g))

    wait_recv(amps.at[0 : MATES - 1], 6)
    every = amps[...]
    line = both_sides(every.reshape(MATES * 4, 128))
    image = summed(mm(gram, jnp.concatenate([line, line], axis=0), NN))
    mates = unpacked(every).reshape(MATES * 8, 128)
    spare = (iota((MATES * 8, 128), 0) & 7) >= MODES
    norm = jnp.sum(jnp.where(spare, mates, mates * image), axis=0, keepdims=True)
    norms[pair] = norm
    for step in PEERS:
        send(norms.at[pair], norms.at[pair], 7, peer(step)[1])

    pl.when(has_before)(lambda: wait_recv(amp_before, 9))
    spread = []
    for f in range(4):
        if f == 0:
            there = unpacked(jnp.where(core == 1, amps[g], amp_before[...]))
            there = jnp.where(has_before | (core == 1), there, 0.0)
        elif f == 1:
            there = jnp.where(core == 1, after, unpacked(amps[4 + g]))
        else:
            there = unpacked(amps[slots_of[1 + f]])
        a_high, a_low = split(jnp.concatenate([own, there], axis=0))
        r_high, r_low = split(jnp.concatenate([own_rf[f], nb_rf[f]], axis=0))
        back = mm(
            jnp.concatenate([a_high, a_low, a_high, a_low], axis=0),
            jnp.concatenate([r_high, r_high, r_low, r_low], axis=0),
            TN,
        )
        spread.append((res_pad[f] + back[:CASES])[:, :FACE])
    next_v[...] = jnp.concatenate(spread, axis=1)
    next_copy = pltpu.make_async_copy(next_v, res_out, out_sem.at[0])
    next_copy.start()
    wait_recv(norms.at[0 : PAIRS - 1], 7)
    ratio = jnp.sum(norms[...], axis=0) / rr_row
    coef_v[...] = jnp.where(row == 0, step_row, ratio)
    coef_copy = pltpu.make_async_copy(coef_v, coef_out, out_sem.at[1])
    coef_copy.start()

    wait_send(own_rf, 0)
    wait_send(rows_in.at[0 : PAIRS - 1, 0:MODES], 1)
    wait_send(loads.at[0 : MATES - 1], 2)
    wait_send(own_y, 3)
    wait_send(grams.at[0 : MATES - 1], 4)
    wait_send(parts.at[0 : PAIRS - 1], 5)
    wait_send(amps.at[0 : MATES - 1], 6)
    pl.when(has_next)(lambda: wait_send(amp_before, 9))
    pl.when(core == 0)(lambda: wait_send(got_next, 8))
    wait_send(norms.at[0 : PAIRS - 1], 7)
    next_copy.wait()
    coef_copy.wait()


def update(
    lam_hbm,
    dir_hbm,
    res_hbm,
    coef_hbm,
    sizes_hbm,
    lam_out,
    res_out,
    dir_out,
    coef_v,
    sizes_ref,
    lam_v,
    res_v,
    dir_v,
    sem,
):
    first = [
        pltpu.make_async_copy(sizes_hbm, sizes_ref, sem.at[0]),
        pltpu.make_async_copy(coef_hbm, coef_v, sem.at[1]),
    ]
    ins = [
        pltpu.make_async_copy(src, dst, sem.at[2 + k])
        for k, (src, dst) in enumerate(((dir_hbm, dir_v), (lam_hbm, lam_v), (res_hbm, res_v)))
    ]
    outs = [
        pltpu.make_async_copy(src, dst, sem.at[5 + k])
        for k, (src, dst) in enumerate(((lam_v, lam_out), (res_v, res_out), (dir_v, dir_out)))
    ]
    for one in first + ins:
        one.start()
    first[0].wait()
    flat = iota((1, WIDTH), 1)
    face = face_at(flat, FACE)
    limit = jnp.zeros_like(face)
    for f in range(4):
        limit = jnp.where(face == f, sizes_ref[0, 0, f], limit)
    active = (flat - face * FACE) < limit
    first[1].wait()
    step_size = column_of(coef_v[0:1, :])
    ratio = column_of(coef_v[1:2, :])
    for one in ins[0:2]:
        one.wait()
    dirn = jnp.where(active, dir_v[...], 0.0)
    lam_v[...] = jnp.where(active, lam_v[...], 0.0) + step_size * dirn
    outs[0].start()
    ins[2].wait()
    outs[1].start()
    dir_v[...] = res_v[...] + ratio * dirn
    outs[2].start()
    for one in outs:
        one.wait()


def on_device(
    multipliers,
    residual,
    direction,
    dual_operator,
    rigid_trace,
    coarse_inverse,
    face_sizes,
    slot_order,
):
    field = jax.ShapeDtypeStruct((CASES, WIDTH), F32)
    hbm = pl.BlockSpec(memory_space=pltpu.HBM)
    res_next, coef = pl.pallas_call(
        kernel,
        out_shape=(field, jax.ShapeDtypeStruct((8, 128), F32)),
        in_specs=[hbm] * 7,
        out_specs=[hbm, hbm],
        scratch_shapes=[
            pltpu.VMEM((CASES, WIDTH), F32),
            pltpu.VMEM((8, 128), F32),
            pltpu.VMEM((CASES, WIDTH), F32),
            pltpu.VMEM((CASES, WIDTH), F32),
            pltpu.VMEM((WIDTH, WIDTH), F32),
            pltpu.VMEM((MODES, 1, WIDTH), F32),
            pltpu.VMEM((MODES, COARSE), F32),
            pltpu.VMEM((1, 1, WIDTH), jnp.int32),
            pltpu.SMEM((1, 1, 4), jnp.int32),
            pltpu.VMEM((4 * ROWS, WIDTH), BF16),
            pltpu.VMEM((WIDTH, 256), BF16),
            pltpu.VMEM((4, 8, PAD), F32),
            pltpu.VMEM((4, 8, PAD), F32),
            pltpu.VMEM((4, CASES, PAD), F32),
            pltpu.VMEM((4, CASES, PAD), F32),
            pltpu.VMEM((4, CASES, PAD), F32),
            pltpu.VMEM((PAIRS, 8, 128), F32),
            pltpu.VMEM((PAIRS, 8, 128), F32),
            pltpu.VMEM((MATES, 16, 128), F32),
            pltpu.VMEM((PAIRS, 4, 128), F32),
            pltpu.VMEM((PAIRS, 4, 128), F32),
            pltpu.VMEM((PAIRS, 4, 128), F32),
            pltpu.VMEM((MATES, 8, 128), F32),
            pltpu.VMEM((MATES, 4, 128), F32),
            pltpu.VMEM((4, 128), F32),
            pltpu.VMEM((PAIRS, 1, 128), F32),
            pltpu.SemaphoreType.DMA((7,)),
            pltpu.SemaphoreType.DMA((2,)),
            pltpu.SemaphoreType.DMA((10,)),
            pltpu.SemaphoreType.DMA((10,)),
        ],
        compiler_params=pltpu.CompilerParams(
            collective_id=0, has_side_effects=True, vmem_limit_bytes=62 * 1024 * 1024
        ),
    )(
        residual.reshape(CASES, WIDTH),
        direction.reshape(CASES, WIDTH),
        dual_operator.reshape(WIDTH, WIDTH),
        rigid_trace.transpose(0, 2, 1, 3).reshape(MODES, 1, WIDTH),
        coarse_inverse,
        face_sizes,
        slot_order,
    )
    outs = pl.pallas_call(
        update,
        out_shape=(field, field, field),
        in_specs=[hbm] * 5,
        out_specs=[hbm, hbm, hbm],
        scratch_shapes=[
            pltpu.VMEM((8, 128), F32),
            pltpu.SMEM((1, 1, 4), jnp.int32),
            pltpu.VMEM((CASES, WIDTH), F32),
            pltpu.VMEM((CASES, WIDTH), F32),
            pltpu.VMEM((CASES, WIDTH), F32),
            pltpu.SemaphoreType.DMA((8,)),
        ],
        compiler_params=pltpu.CompilerParams(vmem_limit_bytes=62 * 1024 * 1024),
    )(
        multipliers.reshape(CASES, WIDTH),
        direction.reshape(CASES, WIDTH),
        res_next,
        coef,
        face_sizes,
    )
    return tuple(x[None, None] for x in outs)


def solution(mesh):
    wide = P("sub", "grp", None, None)
    return jax.shard_map(
        on_device,
        mesh=mesh,
        in_specs=(wide, wide, wide, wide, wide, P(("sub", "grp"), None), P("sub", "grp", None), P("sub", "grp", None)),
        out_specs=(wide, wide, wide),
        check_vma=False,
    )
```

```python
import functools

import jax
import jax.numpy as jnp
from jax import lax
from jax.experimental import pallas as pl
from jax.experimental.pallas import tpu as pltpu
from jax.sharding import PartitionSpec as P

MESH = pl.DeviceIdType.MESH
F32 = jnp.float32
BF16 = jnp.bfloat16
NN = (((1,), (0,)), ((), ()))
NT = (((1,), (1,)), ((), ()))
TN = (((0,), (0,)), ((), ()))

CASES = 64
WIDTH = 1200
FACE = 300
PAD = 384
ROWS = 304
WIDE = 4 * PAD
MODES = 6
COARSE = 1536
PAIRS = 32
MATES = 8
BARRIER_AT = 240
PEERS = sorted(
    ((dx, dz) for dx in range(4) for dz in range(8) if dx or dz),
    key=lambda step: -min(step[0], 4 - step[0]) - min(step[1], 8 - step[1]),
)


def split(x):
    high = x.astype(BF16)
    return high, (x - high.astype(F32)).astype(BF16)


def mm(a, b, dims):
    return lax.dot_general(a, b, dims, preferred_element_type=F32)


def iota(shape, dim):
    return lax.broadcasted_iota(jnp.int32, shape, dim)


def face_at(lane, step):
    one = jnp.int32(1)
    zero = jnp.int32(0)
    return (
        jnp.where(lane >= step, one, zero)
        + jnp.where(lane >= 2 * step, one, zero)
        + jnp.where(lane >= 3 * step, one, zero)
    )


def row_of(column):
    eye = iota((CASES, 128), 0) == iota((CASES, 128), 1)
    return jnp.sum(jnp.where(eye, column, 0.0), axis=0, keepdims=True)


def column_of(row):
    eye = iota((CASES, 128), 0) == iota((CASES, 128), 1)
    return jnp.sum(jnp.where(eye, row, 0.0), axis=1, keepdims=True)


def packed(tile):
    left = iota((8, 128), 1) < 64
    return jnp.where(left, tile, pltpu.roll(tile, 4, 0))[0:4]


def unpacked(half):
    return jnp.concatenate([half, pltpu.roll(half, 64, half.ndim - 1)], axis=half.ndim - 2)


def doubled(x):
    return jnp.where(iota(x.shape, 1) < 64, x, pltpu.roll(x, 64, 1))


def lanes_split(x):
    high = x.astype(BF16).astype(F32)
    return jnp.where(iota(x.shape, 1) < 64, high, x - high).astype(BF16)


def both_sides(x):
    other = pltpu.roll(x, 64, 1)
    left = iota(x.shape, 1) < 64
    return jnp.concatenate(
        [lanes_split(jnp.where(left, x, other)), lanes_split(jnp.where(left, other, x))], axis=0
    )


def summed(x):
    return x + pltpu.roll(x, 64, 1)


def kernel(
    res_hbm,
    dir_hbm,
    dual_hbm,
    trace_hbm,
    inv_hbm,
    sizes_hbm,
    order_hbm,
    next_out,
    next_v,
    coef_v,
    res_v,
    dir_v,
    dual_v,
    trace_v,
    inv_v,
    order_ref,
    sizes_ref,
    perm,
    halves,
    own_rf,
    nb_rf,
    res_pad,
    own_y,
    nb_y,
    rows_out,
    rows_in,
    loads,
    parts,
    got,
    got_next,
    grams,
    amps,
    amp_before,
    scalars,
    norms,
    in_sem,
    out_sem,
    send_sem,
    recv_sem,
):
    s = lax.axis_index("sub")
    g = lax.axis_index("grp")
    pair = s // 2
    core = s % 2
    place = core * 4 + g

    copies_in = {}
    for k, (name, src, dst) in enumerate(
        (
            ("sizes", sizes_hbm, sizes_ref),
            ("order", order_hbm, order_ref),
            ("trace", trace_hbm, trace_v),
            ("dir", dir_hbm, dir_v),
            ("inv", inv_hbm, inv_v),
            ("dual", dual_hbm, dual_v),
            ("res", res_hbm, res_v),
        )
    ):
        copies_in[name] = pltpu.make_async_copy(src, dst, in_sem.at[k])
        copies_in[name].start()

    rows_in[...] = jnp.zeros_like(rows_in)
    across = (
        ((s + 63) % 64, g),
        ((s + 1) % 64, g),
        (s, (g + 3) % 4),
        (s, (g + 1) % 4),
    )

    def mate(step):
        other = (place + step) % MATES
        return (pair * 2 + other // 4, other % 4)

    def peer(step):
        dx, dz = step
        other = (pair // 8 + dx) % 4 * 8 + (pair + dz) % 8
        return other, (other * 2 + core, g)

    has_next = (core == 1) & (pair < PAIRS - 1)
    has_before = (core == 0) & (pair > 0)

    barrier = pltpu.get_barrier_semaphore()
    for step in PEERS:
        pl.semaphore_signal(barrier, inc=1, device_id=peer(step)[1], device_id_type=MESH)
    pl.semaphore_signal(
        barrier, inc=1, device_id=((s + 2 * core + 63) % 64, g), device_id_type=MESH
    )

    @pl.when(core == 1)
    def _():
        for step in PEERS:
            other = peer(step)[0]
            pl.semaphore_signal(barrier, inc=1, device_id=(2 * other, g), device_id_type=MESH)

    for step in range(1, MATES):
        pl.semaphore_signal(barrier, inc=1, device_id=mate(step), device_id_type=MESH)

    def send(src, dst, phase, target):
        pltpu.make_async_remote_copy(
            src_ref=src,
            dst_ref=dst,
            send_sem=send_sem.at[phase],
            recv_sem=recv_sem.at[phase],
            device_id=target,
            device_id_type=MESH,
        ).start()

    def wait_recv(ref, phase):
        pltpu.make_async_copy(ref, ref, recv_sem.at[phase]).wait()

    def wait_send(ref, phase):
        pltpu.make_async_copy(ref, ref, send_sem.at[phase]).wait()

    def greeted():
        pl.semaphore_wait(barrier, (PAIRS - 1) * (2 - core) + 1 + MATES - 1)
        for f in range(4):
            send(own_rf.at[f], nb_rf.at[f ^ 1], 0, across[f])
        for step in PEERS:
            other, target = peer(step)
            send(rows_out.at[other, 0:MODES], rows_in.at[pair, 0:MODES], 1, target)

    copies_in["sizes"].wait()
    copies_in["order"].wait()

    def limits(face):
        out = jnp.zeros_like(face)
        for f in range(4):
            out = jnp.where(face == f, sizes_ref[0, 0, f], out)
        return out

    lane = iota((1, WIDE), 1)
    face = face_at(lane, PAD)
    active_pad = (lane - face * PAD) < limits(face)
    sign_pad = jnp.where((face & 1) == 0, -1.0, 1.0)
    mask_pad = jnp.where(active_pad, sign_pad, 0.0)
    lane = iota((1, 4 * ROWS), 1)
    face = face_at(lane, ROWS)
    active_row = (lane - face * ROWS) < limits(face)
    mask_row = jnp.where(active_row, jnp.where((face & 1) == 0, -1.0, 1.0), 0.0)
    left = iota((8, 128), 1) < 64
    row = iota((8, 128), 0)

    order = order_ref[0]
    order = order + (ROWS - FACE) * face_at(order, FACE)
    line = lax.broadcasted_iota(jnp.int16, (ROWS, WIDTH), 0)
    ones = jnp.ones((ROWS, WIDTH), BF16)
    for f in range(4):
        hot = line == jnp.broadcast_to((order - f * ROWS).astype(jnp.int16), (ROWS, WIDTH))
        perm[f * ROWS : (f + 1) * ROWS, :] = jnp.where(hot, ones, jnp.zeros_like(ones))

    copies_in["trace"].wait()
    trace = jnp.concatenate([trace_v[...].reshape(MODES, WIDTH), jnp.zeros((2, WIDTH), F32)], axis=0)
    low = trace - trace.astype(BF16).astype(F32)
    got_rf = mm(jnp.concatenate([trace, low], axis=0).astype(BF16), perm[...], NT)
    got_rf = (got_rf[:8] + got_rf[8:]) * mask_row
    for f in range(4):
        cut = got_rf[:, f * ROWS : (f + 1) * ROWS]
        own_rf[f] = jnp.concatenate([cut, jnp.zeros((8, PAD - ROWS), F32)], axis=1)

    copies_in["inv"].wait()
    rows = jnp.concatenate([inv_v[...], jnp.zeros((2, COARSE), F32)], axis=0)
    rows = jnp.concatenate([jnp.zeros((8, 24), F32), rows, jnp.zeros((8, 104), F32)], axis=1)
    for p in range(PAIRS):
        rows_out[p] = rows[:, 48 * p : 48 * p + 128]

    def padded(x, width):
        gap = jnp.zeros((CASES, width - FACE), F32)
        spread = []
        for f in range(4):
            spread += [x[:, f * FACE : (f + 1) * FACE], gap]
        return jnp.concatenate(spread, axis=1)

    copies_in["dir"].wait()
    high, low = split(padded(dir_v[...], ROWS) * mask_row)
    slots = mm(jnp.concatenate([high, low], axis=0), perm[...], NN)
    slots = slots[:CASES] + slots[CASES:]

    high, low = split(slots)
    both = jnp.concatenate([high, low], axis=0)
    copies_in["dual"].wait()
    for k in range(0, WIDTH, 240):
        if k == BARRIER_AT:
            greeted()
        f_high, f_low = split(dual_v[k : k + 240, :])
        z_high, z_low = split(mm(f_high, both, NT) + mm(f_low, both, NT))
        halves[k : k + 240, 0:128] = z_high
        halves[k : k + 240, 128:256] = z_low

    ys = []
    for f in range(4):
        y = mm(perm[f * ROWS : (f + 1) * ROWS, :], halves[...], NN)
        ys.append(y[:, :128] + y[:, 128:])
    curvature = mm(both, halves[...], NN)
    curvature = curvature[:, :128] + curvature[:, 128:]
    curvature = curvature[:CASES] + curvature[CASES:]
    diagonal = (iota((CASES, 128), 1) & 63) == iota((CASES, 128), 0)
    curv_row = summed(jnp.sum(jnp.where(diagonal, curvature, 0.0), axis=0, keepdims=True))
    copies_in["res"].wait()
    flat = iota((1, WIDTH), 1)
    flat_face = face_at(flat, FACE)
    active = (flat - flat_face * FACE) < limits(flat_face)
    res = jnp.where(active, res_v[...], 0.0)
    rr_row = row_of(0.5 * jnp.sum(res * res, axis=1, keepdims=True))
    wait_recv(nb_rf, 0)
    own_load = jnp.zeros((8, 128), F32)
    nb_load = []
    for f in range(4):
        cut = slice(f * PAD, (f + 1) * PAD)
        nb_rf[f] = jnp.where(active_pad[:, cut], nb_rf[f], 0.0)
        r_high, r_low = split(jnp.concatenate([own_rf[f, :, :ROWS], nb_rf[f, :, :ROWS]], axis=0))
        y_high, y_low = split(ys[f])
        piece = mm(
            jnp.concatenate([r_high, r_low], axis=0), jnp.concatenate([y_high, y_low], axis=1), NN
        )
        piece = piece[:, :128] + piece[:, 128:]
        piece = piece[:16] + piece[16:32]
        if not f & 1:
            piece = -piece
        own_load = own_load + piece[:8]
        nb_load.append(summed(piece[8:]))
    own_load = summed(own_load)
    own_load = jnp.where(row == 6, rr_row, jnp.where(row == 7, curv_row, own_load))
    for f in range(3):
        moved = pltpu.roll(nb_load[3], 6 - 2 * f, 0)
        nb_load[f] = jnp.where(row < MODES, nb_load[f], moved)
    loads[place, 0:8, :] = jnp.where(left, own_load, nb_load[0])
    loads[place, 8:16, :] = jnp.where(left, nb_load[1], nb_load[2])
    for step in range(1, MATES):
        send(loads.at[place], loads.at[place], 2, mate(step))
    for f in range(4):
        y = jnp.transpose(jnp.concatenate([ys[f], jnp.zeros((PAD - ROWS, 128), F32)], axis=0))
        y = (y[:CASES] + y[CASES:]) * mask_pad[:, f * PAD : (f + 1) * PAD]
        own_y[f] = y
        send(own_y.at[f], nb_y.at[f ^ 1], 3, across[f])
    res = padded(res, PAD)
    for f in range(4):
        res_pad[f] = res[:, f * PAD : (f + 1) * PAD]

    col = iota((1, 256), 1)
    mode = col & 7
    tile = 2 * ((col >> 3) & 1) + (col >> 7)
    member = (col >> 4) & 7
    spare = (mode >= MODES) & (tile > 0)
    group = jnp.where(spare, 4, tile)
    mode = jnp.where(spare, 2 * (tile - 1) + mode - MODES, mode)
    d_sub = jnp.where(group == 1, -1, jnp.where(group == 2, 1, 0))
    d_grp = jnp.where(group == 3, -1, jnp.where(group == 4, 1, 0))
    source = ((member >> 2) + d_sub + 1) * 24 + ((member & 3) + d_grp) * MODES + mode
    source = jnp.where(mode < MODES, source, -1)
    pick = jnp.where(iota((128, 256), 0) == source, 1.0, 0.0).astype(BF16)

    slots_of = (
        place,
        core * g + (1 - core) * MATES,
        core * MATES + (1 - core) * (4 + g),
        core * 4 + (g + 3) % 4,
        core * 4 + (g + 1) % 4,
    )
    lane = iota((32, 128), 1)
    line = iota((32, 128), 0)
    mode = 4 * (lane >> 5) + (lane & 3)
    slot = (lane >> 2) & 7
    gram = jnp.zeros((8, 128), F32)
    for f in range(4):
        r_high, r_low = split(own_rf[f])
        n_high, n_low = split(jnp.concatenate([own_rf[f], nb_rf[f]], axis=0))
        piece = mm(
            jnp.concatenate([r_high, r_low], axis=0), jnp.concatenate([n_high, n_low], axis=0), NT
        )
        piece = piece[:8] + piece[8:]
        if f == 1:
            edge = piece[:, 8:16]
        piece_high, piece_low = split(piece)
        wanted = jnp.where((line & 8) == 0, slots_of[0], slots_of[1 + f])
        hot = ((line & 7) == mode) & (mode < MODES) & (slot == wanted)
        piece = mm(
            jnp.concatenate([piece_high, piece_low], axis=0),
            jnp.where(hot, 1.0, 0.0).astype(BF16),
            NN,
        )
        gram = gram + piece[:8] + piece[8:]
    grams[place] = gram

    rows_in[pair] = rows_out[pair]
    wait_recv(rows_in.at[0 : PAIRS - 1, 0:MODES], 1)
    high, low = split(rows_in[...].reshape(PAIRS * 8, 128))
    piece = mm(jnp.concatenate([high, low], axis=0), pick, NN).astype(BF16)
    piece = jnp.concatenate([piece[: PAIRS * 8], piece[PAIRS * 8 :]], axis=1)

    for step in range(1, MATES):
        send(grams.at[place], grams.at[place], 4, mate(step))

    wait_recv(loads.at[0 : MATES - 1], 2)
    every = loads[...]
    total = doubled(jnp.sum(every[:, 0:8, :], axis=0))
    line = both_sides(every.reshape(MATES * 16, 128))
    part = summed(mm(piece, jnp.concatenate([line, line], axis=0), NN))
    part = part.reshape(PAIRS, 8, 128) + jnp.where(row >= MODES, total, 0.0)[None]
    parts[...] = jnp.where(left[None], part, pltpu.roll(part, 4, 1))[:, 0:4, :]
    @pl.when(core == 0)
    def _():
        for step in PEERS:
            other, target = peer(step)
            send(parts.at[other], got_next.at[pair], 8, ((2 * other + 63) % 64, g))
            send(parts.at[other], got.at[pair], 5, target)
        send(parts.at[pair], got_next.at[pair], 8, ((2 * pair + 63) % 64, g))

    @pl.when(core == 1)
    def _():
        for step in PEERS:
            other, target = peer(step)
            send(parts.at[other], got.at[pair], 5, target)

    got[pair] = parts[pair]

    wait_recv(nb_y, 3)
    trace_res = jnp.zeros((8, 128), F32)
    trace_image = jnp.zeros((8, 128), F32)
    for f in range(4):
        image = own_y[f] + jnp.where(active_pad[:, f * PAD : (f + 1) * PAD], nb_y[f], 0.0)
        nb_y[f] = image
        r_high, r_low = split(own_rf[f])
        b_high, b_low = split(jnp.concatenate([res_pad[f], image], axis=0))
        piece = mm(
            jnp.concatenate([r_high, r_low], axis=0),
            jnp.concatenate(
                [b_high[:CASES], b_low[:CASES], b_high[CASES:], b_low[CASES:]], axis=0
            ),
            NT,
        )
        piece = piece[:8] + piece[8:]
        trace_res = trace_res + piece[:, :128]
        trace_image = trace_image + piece[:, 128:]
    trace_res = summed(trace_res)
    trace_image = summed(trace_image)
    wait_recv(grams.at[0 : MATES - 1], 4)
    gram = lanes_split(summed(grams[...].reshape(MATES * 8, 128)))

    wait_recv(got.at[0 : PAIRS - 1], 5)
    amp = doubled(unpacked(jnp.sum(got[...], axis=0)))
    rr_row = amp[6:7, :]
    step_row = rr_row / amp[7:8, :]
    scaled = jnp.where(row < MODES, step_row * amp, 0.0)
    amps[place] = packed(scaled)
    for step in range(1, MATES):
        send(amps.at[place], amps.at[place], 6, mate(step))

    @pl.when(has_next)
    def _():
        send(amps.at[place], amp_before, 9, (2 * pair + 2, g))

    step_size = column_of(step_row)
    square = jnp.zeros((CASES, 128), F32)
    for f in range(4):
        u = res_pad[f] - step_size * nb_y[f]
        res_pad[f] = u
        for k in range(0, PAD, 128):
            square = square + u[:, k : k + 128] * u[:, k : k + 128]
    u_row = row_of(0.5 * jnp.sum(square, axis=1, keepdims=True))
    cross = trace_res - step_row * trace_image
    pl.when(core == 1)(lambda: wait_recv(got_next, 8))
    after = doubled(unpacked(jnp.sum(got_next[...], axis=0)))
    after = jnp.where((row < MODES) & has_next, step_row * after, 0.0)
    for k in range(MODES):
        cross = cross + edge[:, k : k + 1] * after[k : k + 1, :]
    cross = jnp.sum(scaled * cross, axis=0, keepdims=True)
    scalars[place] = doubled(u_row + 2.0 * cross)
    for step in range(1, MATES):
        send(scalars.at[place], scalars.at[place], 10, mate(step))

    wait_recv(amps.at[0 : MATES - 1], 6)
    every = amps[...]
    line = both_sides(every.reshape(MATES * 4, 128))
    image = summed(mm(gram, jnp.concatenate([line, line], axis=0), NN))
    mates = unpacked(every).reshape(MATES * 8, 128)
    norm = jnp.sum(mates * image, axis=0, keepdims=True)
    wait_recv(scalars.at[0 : MATES - 1], 10)
    norms[pair] = norm + jnp.sum(scalars[...], axis=0)
    for step in PEERS:
        send(norms.at[pair], norms.at[pair], 7, peer(step)[1])

    pl.when(has_before)(lambda: wait_recv(amp_before, 9))
    spread = []
    for f in range(4):
        if f == 0:
            there = unpacked(jnp.where(core == 1, amps[g], amp_before[...]))
            there = jnp.where(has_before | (core == 1), there, 0.0)
        elif f == 1:
            there = jnp.where(core == 1, after, unpacked(amps[4 + g]))
        else:
            there = unpacked(amps[slots_of[1 + f]])
        a_high, a_low = split(jnp.concatenate([scaled, there], axis=0))
        r_high, r_low = split(jnp.concatenate([own_rf[f], nb_rf[f]], axis=0))
        back = mm(
            jnp.concatenate([a_high, a_low, a_high, a_low], axis=0),
            jnp.concatenate([r_high, r_high, r_low, r_low], axis=0),
            TN,
        )
        spread.append((res_pad[f] + back[:CASES])[:, :FACE])
    next_v[...] = jnp.concatenate(spread, axis=1)
    next_copy = pltpu.make_async_copy(next_v, next_out.at[0:CASES], out_sem.at[0])
    next_copy.start()
    wait_recv(norms.at[0 : PAIRS - 1], 7)
    ratio = jnp.sum(norms[...], axis=0) / rr_row
    coef_v[...] = jnp.where(row == 0, step_row, ratio)
    coef_copy = pltpu.make_async_copy(coef_v, next_out.at[CASES:, 0:128], out_sem.at[1])
    coef_copy.start()

    wait_send(own_rf, 0)
    wait_send(rows_in.at[0 : PAIRS - 1, 0:MODES], 1)
    wait_send(loads.at[0 : MATES - 1], 2)
    wait_send(own_y, 3)
    wait_send(grams.at[0 : MATES - 1], 4)
    wait_send(parts.at[0 : PAIRS - 1], 5)
    wait_send(amps.at[0 : MATES - 1], 6)
    wait_send(scalars.at[0 : MATES - 1], 10)
    pl.when(has_next)(lambda: wait_send(amp_before, 9))
    pl.when(core == 0)(lambda: wait_send(got_next, 8))
    wait_send(norms.at[0 : PAIRS - 1], 7)
    next_copy.wait()
    coef_copy.wait()


def update(
    lam_ref,
    dir_ref,
    res_hbm,
    sizes_hbm,
    lam_out,
    res_out,
    dir_out,
    coef_v,
    sizes_ref,
    lam_v,
    res_v,
    dir_v,
    sem,
):
    ins = [
        pltpu.make_async_copy(src, dst, sem.at[k])
        for k, (src, dst) in enumerate(
            ((sizes_hbm, sizes_ref), (res_hbm.at[CASES:, 0:128], coef_v), (res_hbm.at[0:CASES], res_v))
        )
    ]
    outs = [
        pltpu.make_async_copy(src, dst, sem.at[3 + k])
        for k, (src, dst) in enumerate(((lam_v, lam_out), (res_v, res_out), (dir_v, dir_out)))
    ]
    for one in ins:
        one.start()
    ins[0].wait()
    flat = iota((1, WIDTH), 1)
    face = face_at(flat, FACE)
    limit = jnp.zeros_like(face)
    for f in range(4):
        limit = jnp.where(face == f, sizes_ref[0, 0, f], limit)
    active = (flat - face * FACE) < limit
    dirn = jnp.where(active, dir_ref[...], 0.0)
    ins[1].wait()
    step_size = column_of(coef_v[0:1, :])
    ratio = column_of(coef_v[1:2, :])
    lam_v[...] = jnp.where(active, lam_ref[...], 0.0) + step_size * dirn
    outs[0].start()
    ins[2].wait()
    outs[1].start()
    dir_v[...] = res_v[...] + ratio * dirn
    outs[2].start()
    for one in outs:
        one.wait()


def on_device(
    multipliers,
    residual,
    direction,
    dual_operator,
    rigid_trace,
    coarse_inverse,
    face_sizes,
    slot_order,
):
    field = jax.ShapeDtypeStruct((CASES, WIDTH), F32)
    hbm = pl.BlockSpec(memory_space=pltpu.HBM)
    vmem = pl.BlockSpec(memory_space=pltpu.VMEM)
    res_next = pl.pallas_call(
        kernel,
        out_shape=jax.ShapeDtypeStruct((CASES + 8, WIDTH), F32),
        in_specs=[hbm] * 7,
        out_specs=hbm,
        scratch_shapes=[
            pltpu.VMEM((CASES, WIDTH), F32),
            pltpu.VMEM((8, 128), F32),
            pltpu.VMEM((CASES, WIDTH), F32),
            pltpu.VMEM((CASES, WIDTH), F32),
            pltpu.VMEM((WIDTH, WIDTH), F32),
            pltpu.VMEM((MODES, 1, WIDTH), F32),
            pltpu.VMEM((MODES, COARSE), F32),
            pltpu.VMEM((1, 1, WIDTH), jnp.int32),
            pltpu.SMEM((1, 1, 4), jnp.int32),
            pltpu.VMEM((4 * ROWS, WIDTH), BF16),
            pltpu.VMEM((WIDTH, 256), BF16),
            pltpu.VMEM((4, 8, PAD), F32),
            pltpu.VMEM((4, 8, PAD), F32),
            pltpu.VMEM((4, CASES, PAD), F32),
            pltpu.VMEM((4, CASES, PAD), F32),
            pltpu.VMEM((4, CASES, PAD), F32),
            pltpu.VMEM((PAIRS, 8, 128), F32),
            pltpu.VMEM((PAIRS, 8, 128), F32),
            pltpu.VMEM((MATES, 16, 128), F32),
            pltpu.VMEM((PAIRS, 4, 128), F32),
            pltpu.VMEM((PAIRS, 4, 128), F32),
            pltpu.VMEM((PAIRS, 4, 128), F32),
            pltpu.VMEM((MATES, 8, 128), F32),
            pltpu.VMEM((MATES, 4, 128), F32),
            pltpu.VMEM((4, 128), F32),
            pltpu.VMEM((MATES, 1, 128), F32),
            pltpu.VMEM((PAIRS, 1, 128), F32),
            pltpu.SemaphoreType.DMA((7,)),
            pltpu.SemaphoreType.DMA((2,)),
            pltpu.SemaphoreType.DMA((11,)),
            pltpu.SemaphoreType.DMA((11,)),
        ],
        compiler_params=pltpu.CompilerParams(
            collective_id=0, has_side_effects=True, vmem_limit_bytes=62 * 1024 * 1024
        ),
    )(
        residual.reshape(CASES, WIDTH),
        direction.reshape(CASES, WIDTH),
        dual_operator.reshape(WIDTH, WIDTH),
        rigid_trace.transpose(0, 2, 1, 3).reshape(MODES, 1, WIDTH),
        coarse_inverse,
        face_sizes,
        slot_order,
    )
    outs = pl.pallas_call(
        update,
        out_shape=(field, field, field),
        in_specs=[vmem, vmem, hbm, hbm],
        out_specs=[hbm, hbm, hbm],
        scratch_shapes=[
            pltpu.VMEM((8, 128), F32),
            pltpu.SMEM((1, 1, 4), jnp.int32),
            pltpu.VMEM((CASES, WIDTH), F32),
            pltpu.VMEM((CASES, WIDTH), F32),
            pltpu.VMEM((CASES, WIDTH), F32),
            pltpu.SemaphoreType.DMA((6,)),
        ],
        compiler_params=pltpu.CompilerParams(vmem_limit_bytes=55600000),
    )(
        multipliers.reshape(CASES, WIDTH),
        direction.reshape(CASES, WIDTH),
        res_next,
        face_sizes,
    )
    return tuple(x[None, None] for x in outs)


def solution(mesh):
    wide = P("sub", "grp", None, None)
    return jax.shard_map(
        on_device,
        mesh=mesh,
        in_specs=(wide, wide, wide, wide, wide, P(("sub", "grp"), None), P("sub", "grp", None), P("sub", "grp", None)),
        out_specs=(wide, wide, wide),
        check_vma=False,
    )
```

```python
import functools

import jax
import jax.numpy as jnp
from jax import lax
from jax.experimental import pallas as pl
from jax.experimental.pallas import tpu as pltpu
from jax.sharding import PartitionSpec as P

MESH = pl.DeviceIdType.MESH
F32 = jnp.float32
BF16 = jnp.bfloat16
NN = (((1,), (0,)), ((), ()))
NT = (((1,), (1,)), ((), ()))
TN = (((0,), (0,)), ((), ()))

CASES = 64
WIDTH = 1200
FACE = 300
PAD = 384
ROWS = 304
WIDE = 4 * PAD
MODES = 6
COARSE = 1536
PAIRS = 32
MATES = 8
BARRIER_AT = 240
PEERS = sorted(
    ((dx, dz) for dx in range(4) for dz in range(8) if dx or dz),
    key=lambda step: -min(step[0], 4 - step[0]) - min(step[1], 8 - step[1]),
)


def split(x):
    high = x.astype(BF16)
    return high, (x - high.astype(F32)).astype(BF16)


def mm(a, b, dims):
    return lax.dot_general(a, b, dims, preferred_element_type=F32)


def iota(shape, dim):
    return lax.broadcasted_iota(jnp.int32, shape, dim)


def face_at(lane, step):
    one = jnp.int32(1)
    zero = jnp.int32(0)
    return (
        jnp.where(lane >= step, one, zero)
        + jnp.where(lane >= 2 * step, one, zero)
        + jnp.where(lane >= 3 * step, one, zero)
    )


def row_of(column):
    eye = iota((CASES, 128), 0) == iota((CASES, 128), 1)
    return jnp.sum(jnp.where(eye, column, 0.0), axis=0, keepdims=True)


def column_of(row):
    eye = iota((CASES, 128), 0) == iota((CASES, 128), 1)
    return jnp.sum(jnp.where(eye, row, 0.0), axis=1, keepdims=True)


def packed(tile):
    left = iota((8, 128), 1) < 64
    return jnp.where(left, tile, pltpu.roll(tile, 4, 0))[0:4]


def unpacked(half):
    return jnp.concatenate([half, pltpu.roll(half, 64, half.ndim - 1)], axis=half.ndim - 2)


def doubled(x):
    return jnp.where(iota(x.shape, 1) < 64, x, pltpu.roll(x, 64, 1))


def lanes_split(x):
    high = x.astype(BF16).astype(F32)
    return jnp.where(iota(x.shape, 1) < 64, high, x - high).astype(BF16)


def both_sides(x):
    other = pltpu.roll(x, 64, 1)
    left = iota(x.shape, 1) < 64
    return jnp.concatenate(
        [lanes_split(jnp.where(left, x, other)), lanes_split(jnp.where(left, other, x))], axis=0
    )


def summed(x):
    return x + pltpu.roll(x, 64, 1)


def kernel(
    res_hbm,
    dir_hbm,
    dual_hbm,
    trace_hbm,
    inv_hbm,
    sizes_hbm,
    order_hbm,
    next_out,
    next_v,
    coef_v,
    res_v,
    dir_v,
    dual_v,
    trace_v,
    inv_v,
    order_ref,
    sizes_ref,
    perm,
    halves,
    own_rf,
    nb_rf,
    res_pad,
    own_y,
    nb_y,
    rows_out,
    rows_in,
    loads,
    parts,
    got,
    got_next,
    grams,
    amps,
    amp_before,
    scalars,
    norms,
    in_sem,
    out_sem,
    send_sem,
    recv_sem,
):
    s = lax.axis_index("sub")
    g = lax.axis_index("grp")
    pair = s // 2
    core = s % 2
    place = core * 4 + g

    copies_in = {}
    for k, (name, src, dst) in enumerate(
        (
            ("sizes", sizes_hbm, sizes_ref),
            ("order", order_hbm, order_ref),
            ("trace", trace_hbm, trace_v),
            ("dir", dir_hbm, dir_v),
            ("inv", inv_hbm, inv_v),
            ("dual", dual_hbm, dual_v),
            ("res", res_hbm, res_v),
        )
    ):
        copies_in[name] = pltpu.make_async_copy(src, dst, in_sem.at[k])
        copies_in[name].start()

    rows_in[...] = jnp.zeros_like(rows_in)
    across = (
        ((s + 63) % 64, g),
        ((s + 1) % 64, g),
        (s, (g + 3) % 4),
        (s, (g + 1) % 4),
    )

    def mate(step):
        other = (place + step) % MATES
        return (pair * 2 + other // 4, other % 4)

    def peer(step):
        dx, dz = step
        other = (pair // 8 + dx) % 4 * 8 + (pair + dz) % 8
        return other, (other * 2 + core, g)

    has_next = (core == 1) & (pair < PAIRS - 1)
    has_before = (core == 0) & (pair > 0)

    barrier = pltpu.get_barrier_semaphore()
    for step in PEERS:
        pl.semaphore_signal(barrier, inc=1, device_id=peer(step)[1], device_id_type=MESH)
    pl.semaphore_signal(
        barrier, inc=1, device_id=((s + 2 * core + 63) % 64, g), device_id_type=MESH
    )

    for step in range(1, MATES):
        pl.semaphore_signal(barrier, inc=1, device_id=mate(step), device_id_type=MESH)

    def send(src, dst, phase, target):
        pltpu.make_async_remote_copy(
            src_ref=src,
            dst_ref=dst,
            send_sem=send_sem.at[phase],
            recv_sem=recv_sem.at[phase],
            device_id=target,
            device_id_type=MESH,
        ).start()

    def wait_recv(ref, phase):
        pltpu.make_async_copy(ref, ref, recv_sem.at[phase]).wait()

    def wait_send(ref, phase):
        pltpu.make_async_copy(ref, ref, send_sem.at[phase]).wait()

    def greeted():
        pl.semaphore_wait(barrier, PAIRS - 1 + 1 + MATES - 1)
        for f in range(4):
            send(own_rf.at[f], nb_rf.at[f ^ 1], 0, across[f])
        for step in PEERS:
            other, target = peer(step)
            send(rows_out.at[other, 0:MODES], rows_in.at[pair, 0:MODES], 1, target)

    copies_in["sizes"].wait()
    copies_in["order"].wait()

    def limits(face):
        out = jnp.zeros_like(face)
        for f in range(4):
            out = jnp.where(face == f, sizes_ref[0, 0, f], out)
        return out

    lane = iota((1, WIDE), 1)
    face = face_at(lane, PAD)
    active_pad = (lane - face * PAD) < limits(face)
    sign_pad = jnp.where((face & 1) == 0, -1.0, 1.0)
    mask_pad = jnp.where(active_pad, sign_pad, 0.0)
    lane = iota((1, 4 * ROWS), 1)
    face = face_at(lane, ROWS)
    active_row = (lane - face * ROWS) < limits(face)
    mask_row = jnp.where(active_row, jnp.where((face & 1) == 0, -1.0, 1.0), 0.0)
    left = iota((8, 128), 1) < 64
    row = iota((8, 128), 0)

    order = order_ref[0]
    order = order + (ROWS - FACE) * face_at(order, FACE)
    line = lax.broadcasted_iota(jnp.int16, (ROWS, WIDTH), 0)
    ones = jnp.ones((ROWS, WIDTH), BF16)
    for f in range(4):
        hot = line == jnp.broadcast_to((order - f * ROWS).astype(jnp.int16), (ROWS, WIDTH))
        perm[f * ROWS : (f + 1) * ROWS, :] = jnp.where(hot, ones, jnp.zeros_like(ones))

    copies_in["trace"].wait()
    trace = jnp.concatenate([trace_v[...].reshape(MODES, WIDTH), jnp.zeros((2, WIDTH), F32)], axis=0)
    low = trace - trace.astype(BF16).astype(F32)
    got_rf = mm(jnp.concatenate([trace, low], axis=0).astype(BF16), perm[...], NT)
    got_rf = (got_rf[:8] + got_rf[8:]) * mask_row
    for f in range(4):
        cut = got_rf[:, f * ROWS : (f + 1) * ROWS]
        own_rf[f] = jnp.concatenate([cut, jnp.zeros((8, PAD - ROWS), F32)], axis=1)

    copies_in["inv"].wait()
    rows = jnp.concatenate([inv_v[...], jnp.zeros((2, COARSE), F32)], axis=0)
    rows = jnp.concatenate([jnp.zeros((8, 24), F32), rows, jnp.zeros((8, 104), F32)], axis=1)
    for p in range(PAIRS):
        rows_out[p] = rows[:, 48 * p : 48 * p + 128]

    def padded(x, width):
        gap = jnp.zeros((CASES, width - FACE), F32)
        spread = []
        for f in range(4):
            spread += [x[:, f * FACE : (f + 1) * FACE], gap]
        return jnp.concatenate(spread, axis=1)

    copies_in["dir"].wait()
    high, low = split(padded(dir_v[...], ROWS) * mask_row)
    slots = mm(jnp.concatenate([high, low], axis=0), perm[...], NN)
    slots = slots[:CASES] + slots[CASES:]

    high, low = split(slots)
    both = jnp.concatenate([high, low], axis=0)
    copies_in["dual"].wait()
    for k in range(0, WIDTH, 240):
        if k == BARRIER_AT:
            greeted()
        f_high, f_low = split(dual_v[k : k + 240, :])
        z_high, z_low = split(mm(f_high, both, NT) + mm(f_low, both, NT))
        halves[k : k + 240, 0:128] = z_high
        halves[k : k + 240, 128:256] = z_low

    ys = []
    for f in range(4):
        y = mm(perm[f * ROWS : (f + 1) * ROWS, :], halves[...], NN)
        ys.append(y[:, :128] + y[:, 128:])
    curvature = mm(both, halves[...], NN)
    curvature = curvature[:, :128] + curvature[:, 128:]
    curvature = curvature[:CASES] + curvature[CASES:]
    diagonal = (iota((CASES, 128), 1) & 63) == iota((CASES, 128), 0)
    curv_row = summed(jnp.sum(jnp.where(diagonal, curvature, 0.0), axis=0, keepdims=True))
    copies_in["res"].wait()
    flat = iota((1, WIDTH), 1)
    flat_face = face_at(flat, FACE)
    active = (flat - flat_face * FACE) < limits(flat_face)
    res = jnp.where(active, res_v[...], 0.0)
    rr_row = row_of(0.5 * jnp.sum(res * res, axis=1, keepdims=True))
    wait_recv(nb_rf, 0)
    own_load = jnp.zeros((8, 128), F32)
    nb_load = []
    for f in range(4):
        cut = slice(f * PAD, (f + 1) * PAD)
        nb_rf[f] = jnp.where(active_pad[:, cut], nb_rf[f], 0.0)
        r_high, r_low = split(jnp.concatenate([own_rf[f, :, :ROWS], nb_rf[f, :, :ROWS]], axis=0))
        y_high, y_low = split(ys[f])
        piece = mm(
            jnp.concatenate([r_high, r_low], axis=0), jnp.concatenate([y_high, y_low], axis=1), NN
        )
        piece = piece[:, :128] + piece[:, 128:]
        piece = piece[:16] + piece[16:32]
        if not f & 1:
            piece = -piece
        own_load = own_load + piece[:8]
        nb_load.append(summed(piece[8:]))
    own_load = summed(own_load)
    own_load = jnp.where(row == 6, rr_row, jnp.where(row == 7, curv_row, own_load))
    for f in range(3):
        moved = pltpu.roll(nb_load[3], 6 - 2 * f, 0)
        nb_load[f] = jnp.where(row < MODES, nb_load[f], moved)
    loads[place, 0:8, :] = jnp.where(left, own_load, nb_load[0])
    loads[place, 8:16, :] = jnp.where(left, nb_load[1], nb_load[2])
    for step in range(1, MATES):
        send(loads.at[place], loads.at[place], 2, mate(step))
    for f in range(4):
        y = jnp.transpose(jnp.concatenate([ys[f], jnp.zeros((PAD - ROWS, 128), F32)], axis=0))
        y = (y[:CASES] + y[CASES:]) * mask_pad[:, f * PAD : (f + 1) * PAD]
        own_y[f] = y
        send(own_y.at[f], nb_y.at[f ^ 1], 3, across[f])
    res = padded(res, PAD)
    for f in range(4):
        res_pad[f] = res[:, f * PAD : (f + 1) * PAD]

    col = iota((1, 256), 1)
    mode = col & 7
    tile = 2 * ((col >> 3) & 1) + (col >> 7)
    member = (col >> 4) & 7
    spare = (mode >= MODES) & (tile > 0)
    group = jnp.where(spare, 4, tile)
    mode = jnp.where(spare, 2 * (tile - 1) + mode - MODES, mode)
    d_sub = jnp.where(group == 1, -1, jnp.where(group == 2, 1, 0))
    d_grp = jnp.where(group == 3, -1, jnp.where(group == 4, 1, 0))
    source = ((member >> 2) + d_sub + 1) * 24 + ((member & 3) + d_grp) * MODES + mode
    source = jnp.where(mode < MODES, source, -1)
    pick = jnp.where(iota((128, 256), 0) == source, 1.0, 0.0).astype(BF16)

    slots_of = (
        place,
        core * g + (1 - core) * MATES,
        core * MATES + (1 - core) * (4 + g),
        core * 4 + (g + 3) % 4,
        core * 4 + (g + 1) % 4,
    )
    lane = iota((32, 128), 1)
    line = iota((32, 128), 0)
    mode = 4 * (lane >> 5) + (lane & 3)
    slot = (lane >> 2) & 7
    gram = jnp.zeros((8, 128), F32)
    for f in range(4):
        r_high, r_low = split(own_rf[f])
        n_high, n_low = split(jnp.concatenate([own_rf[f], nb_rf[f]], axis=0))
        piece = mm(
            jnp.concatenate([r_high, r_low], axis=0), jnp.concatenate([n_high, n_low], axis=0), NT
        )
        piece = piece[:8] + piece[8:]
        if f == 1:
            edge = piece[:, 8:16]
        piece_high, piece_low = split(piece)
        wanted = jnp.where((line & 8) == 0, slots_of[0], slots_of[1 + f])
        hot = ((line & 7) == mode) & (mode < MODES) & (slot == wanted)
        piece = mm(
            jnp.concatenate([piece_high, piece_low], axis=0),
            jnp.where(hot, 1.0, 0.0).astype(BF16),
            NN,
        )
        gram = gram + piece[:8] + piece[8:]
    grams[place] = gram

    rows_in[pair] = rows_out[pair]
    wait_recv(rows_in.at[0 : PAIRS - 1, 0:MODES], 1)
    high, low = split(rows_in[...].reshape(PAIRS * 8, 128))
    piece = mm(jnp.concatenate([high, low], axis=0), pick, NN).astype(BF16)
    piece = jnp.concatenate([piece[: PAIRS * 8], piece[PAIRS * 8 :]], axis=1)

    for step in range(1, MATES):
        send(grams.at[place], grams.at[place], 4, mate(step))

    wait_recv(loads.at[0 : MATES - 1], 2)
    every = loads[...]
    total = doubled(jnp.sum(every[:, 0:8, :], axis=0))
    line = both_sides(every.reshape(MATES * 16, 128))
    part = summed(mm(piece, jnp.concatenate([line, line], axis=0), NN))
    part = part.reshape(PAIRS, 8, 128) + jnp.where(row >= MODES, total, 0.0)[None]
    parts[...] = jnp.where(left[None], part, pltpu.roll(part, 4, 1))[:, 0:4, :]
    @pl.when(core == 0)
    def _():
        for step in PEERS:
            other, target = peer(step)
            send(parts.at[other], got_next.at[pair], 8, ((2 * other + 63) % 64, g))
            send(parts.at[other], got.at[pair], 5, target)
        send(parts.at[pair], got_next.at[pair], 8, ((2 * pair + 63) % 64, g))

    @pl.when(core == 1)
    def _():
        for step in PEERS:
            other, target = peer(step)
            send(parts.at[other], got.at[pair], 5, target)

    got[pair] = parts[pair]

    wait_recv(nb_y, 3)
    trace_res = jnp.zeros((8, 128), F32)
    trace_image = jnp.zeros((8, 128), F32)
    for f in range(4):
        image = own_y[f] + jnp.where(active_pad[:, f * PAD : (f + 1) * PAD], nb_y[f], 0.0)
        nb_y[f] = image
        r_high, r_low = split(own_rf[f])
        b_high, b_low = split(jnp.concatenate([res_pad[f], image], axis=0))
        piece = mm(
            jnp.concatenate([r_high, r_low], axis=0),
            jnp.concatenate(
                [b_high[:CASES], b_low[:CASES], b_high[CASES:], b_low[CASES:]], axis=0
            ),
            NT,
        )
        piece = piece[:8] + piece[8:]
        trace_res = trace_res + piece[:, :128]
        trace_image = trace_image + piece[:, 128:]
    trace_res = summed(trace_res)
    trace_image = summed(trace_image)
    wait_recv(grams.at[0 : MATES - 1], 4)
    gram = lanes_split(summed(grams[...].reshape(MATES * 8, 128)))

    wait_recv(got.at[0 : PAIRS - 1], 5)
    amp = doubled(unpacked(jnp.sum(got[...], axis=0)))
    rr_row = amp[6:7, :]
    step_row = rr_row / amp[7:8, :]
    scaled = jnp.where(row < MODES, step_row * amp, 0.0)
    amps[place] = packed(scaled)
    for step in range(1, MATES):
        send(amps.at[place], amps.at[place], 6, mate(step))

    @pl.when(has_next)
    def _():
        send(amps.at[place], amp_before, 9, (2 * pair + 2, g))

    step_size = column_of(step_row)
    square = jnp.zeros((CASES, 128), F32)
    for f in range(4):
        u = res_pad[f] - step_size * nb_y[f]
        res_pad[f] = u
        for k in range(0, PAD, 128):
            square = square + u[:, k : k + 128] * u[:, k : k + 128]
    u_row = row_of(0.5 * jnp.sum(square, axis=1, keepdims=True))
    cross = trace_res - step_row * trace_image
    pl.when(core == 1)(lambda: wait_recv(got_next, 8))
    after = doubled(unpacked(jnp.sum(got_next[...], axis=0)))
    after = jnp.where((row < MODES) & has_next, step_row * after, 0.0)
    for k in range(MODES):
        cross = cross + edge[:, k : k + 1] * after[k : k + 1, :]
    cross = jnp.sum(scaled * cross, axis=0, keepdims=True)
    scalars[place] = doubled(u_row + 2.0 * cross)
    for step in range(1, MATES):
        send(scalars.at[place], scalars.at[place], 10, mate(step))

    wait_recv(amps.at[0 : MATES - 1], 6)
    every = amps[...]
    line = both_sides(every.reshape(MATES * 4, 128))
    image = summed(mm(gram, jnp.concatenate([line, line], axis=0), NN))
    mates = unpacked(every).reshape(MATES * 8, 128)
    norm = jnp.sum(mates * image, axis=0, keepdims=True)
    wait_recv(scalars.at[0 : MATES - 1], 10)
    norms[pair] = norm + jnp.sum(scalars[...], axis=0)
    for step in PEERS:
        send(norms.at[pair], norms.at[pair], 7, peer(step)[1])

    pl.when(has_before)(lambda: wait_recv(amp_before, 9))
    spread = []
    for f in range(4):
        if f == 0:
            there = unpacked(jnp.where(core == 1, amps[g], amp_before[...]))
            there = jnp.where(has_before | (core == 1), there, 0.0)
        elif f == 1:
            there = jnp.where(core == 1, after, unpacked(amps[4 + g]))
        else:
            there = unpacked(amps[slots_of[1 + f]])
        a_high, a_low = split(jnp.concatenate([scaled, there], axis=0))
        r_high, r_low = split(jnp.concatenate([own_rf[f], nb_rf[f]], axis=0))
        back = mm(
            jnp.concatenate([a_high, a_low, a_high, a_low], axis=0),
            jnp.concatenate([r_high, r_high, r_low, r_low], axis=0),
            TN,
        )
        spread.append((res_pad[f] + back[:CASES])[:, :FACE])
    next_v[...] = jnp.concatenate(spread, axis=1)
    next_copy = pltpu.make_async_copy(next_v, next_out.at[0:CASES], out_sem.at[0])
    next_copy.start()
    wait_recv(norms.at[0 : PAIRS - 1], 7)
    ratio = jnp.sum(norms[...], axis=0) / rr_row
    coef_v[...] = jnp.where(row == 0, step_row, ratio)
    coef_copy = pltpu.make_async_copy(coef_v, next_out.at[CASES:, 0:128], out_sem.at[1])
    coef_copy.start()

    wait_send(own_rf, 0)
    wait_send(rows_in.at[0 : PAIRS - 1, 0:MODES], 1)
    wait_send(loads.at[0 : MATES - 1], 2)
    wait_send(own_y, 3)
    wait_send(grams.at[0 : MATES - 1], 4)
    wait_send(parts.at[0 : PAIRS - 1], 5)
    wait_send(amps.at[0 : MATES - 1], 6)
    wait_send(scalars.at[0 : MATES - 1], 10)
    pl.when(has_next)(lambda: wait_send(amp_before, 9))
    pl.when(core == 0)(lambda: wait_send(got_next, 8))
    wait_send(norms.at[0 : PAIRS - 1], 7)
    next_copy.wait()
    coef_copy.wait()


def update(
    lam_ref,
    dir_ref,
    res_hbm,
    sizes_hbm,
    lam_out,
    res_out,
    dir_out,
    coef_v,
    sizes_ref,
    lam_v,
    res_v,
    dir_v,
    sem,
):
    ins = [
        pltpu.make_async_copy(src, dst, sem.at[k])
        for k, (src, dst) in enumerate(
            ((sizes_hbm, sizes_ref), (res_hbm.at[CASES:, 0:128], coef_v), (res_hbm.at[0:CASES], res_v))
        )
    ]
    outs = [
        pltpu.make_async_copy(src, dst, sem.at[3 + k])
        for k, (src, dst) in enumerate(((lam_v, lam_out), (res_v, res_out), (dir_v, dir_out)))
    ]
    for one in ins:
        one.start()
    ins[0].wait()
    flat = iota((1, WIDTH), 1)
    face = face_at(flat, FACE)
    limit = jnp.zeros_like(face)
    for f in range(4):
        limit = jnp.where(face == f, sizes_ref[0, 0, f], limit)
    active = (flat - face * FACE) < limit
    dirn = jnp.where(active, dir_ref[...], 0.0)
    ins[1].wait()
    step_size = column_of(coef_v[0:1, :])
    ratio = column_of(coef_v[1:2, :])
    lam_v[...] = jnp.where(active, lam_ref[...], 0.0) + step_size * dirn
    outs[0].start()
    ins[2].wait()
    outs[1].start()
    dir_v[...] = res_v[...] + ratio * dirn
    outs[2].start()
    for one in outs:
        one.wait()


def on_device(
    multipliers,
    residual,
    direction,
    dual_operator,
    rigid_trace,
    coarse_inverse,
    face_sizes,
    slot_order,
):
    field = jax.ShapeDtypeStruct((CASES, WIDTH), F32)
    hbm = pl.BlockSpec(memory_space=pltpu.HBM)
    vmem = pl.BlockSpec(memory_space=pltpu.VMEM)
    res_next = pl.pallas_call(
        kernel,
        out_shape=jax.ShapeDtypeStruct((CASES + 8, WIDTH), F32),
        in_specs=[hbm] * 7,
        out_specs=hbm,
        scratch_shapes=[
            pltpu.VMEM((CASES, WIDTH), F32),
            pltpu.VMEM((8, 128), F32),
            pltpu.VMEM((CASES, WIDTH), F32),
            pltpu.VMEM((CASES, WIDTH), F32),
            pltpu.VMEM((WIDTH, WIDTH), F32),
            pltpu.VMEM((MODES, 1, WIDTH), F32),
            pltpu.VMEM((MODES, COARSE), F32),
            pltpu.VMEM((1, 1, WIDTH), jnp.int32),
            pltpu.SMEM((1, 1, 4), jnp.int32),
            pltpu.VMEM((4 * ROWS, WIDTH), BF16),
            pltpu.VMEM((WIDTH, 256), BF16),
            pltpu.VMEM((4, 8, PAD), F32),
            pltpu.VMEM((4, 8, PAD), F32),
            pltpu.VMEM((4, CASES, PAD), F32),
            pltpu.VMEM((4, CASES, PAD), F32),
            pltpu.VMEM((4, CASES, PAD), F32),
            pltpu.VMEM((PAIRS, 8, 128), F32),
            pltpu.VMEM((PAIRS, 8, 128), F32),
            pltpu.VMEM((MATES, 16, 128), F32),
            pltpu.VMEM((PAIRS, 4, 128), F32),
            pltpu.VMEM((PAIRS, 4, 128), F32),
            pltpu.VMEM((PAIRS, 4, 128), F32),
            pltpu.VMEM((MATES, 8, 128), F32),
            pltpu.VMEM((MATES, 4, 128), F32),
            pltpu.VMEM((4, 128), F32),
            pltpu.VMEM((MATES, 1, 128), F32),
            pltpu.VMEM((PAIRS, 1, 128), F32),
            pltpu.SemaphoreType.DMA((7,)),
            pltpu.SemaphoreType.DMA((2,)),
            pltpu.SemaphoreType.DMA((11,)),
            pltpu.SemaphoreType.DMA((11,)),
        ],
        compiler_params=pltpu.CompilerParams(
            collective_id=0, has_side_effects=True, vmem_limit_bytes=62 * 1024 * 1024
        ),
    )(
        residual.reshape(CASES, WIDTH),
        direction.reshape(CASES, WIDTH),
        dual_operator.reshape(WIDTH, WIDTH),
        rigid_trace.transpose(0, 2, 1, 3).reshape(MODES, 1, WIDTH),
        coarse_inverse,
        face_sizes,
        slot_order,
    )
    outs = pl.pallas_call(
        update,
        out_shape=(field, field, field),
        in_specs=[vmem, vmem, hbm, hbm],
        out_specs=[hbm, hbm, hbm],
        scratch_shapes=[
            pltpu.VMEM((8, 128), F32),
            pltpu.SMEM((1, 1, 4), jnp.int32),
            pltpu.VMEM((CASES, WIDTH), F32),
            pltpu.VMEM((CASES, WIDTH), F32),
            pltpu.VMEM((CASES, WIDTH), F32),
            pltpu.SemaphoreType.DMA((6,)),
        ],
        compiler_params=pltpu.CompilerParams(vmem_limit_bytes=55600000),
    )(
        multipliers.reshape(CASES, WIDTH),
        direction.reshape(CASES, WIDTH),
        res_next,
        face_sizes,
    )
    return tuple(x[None, None] for x in outs)


def solution(mesh):
    wide = P("sub", "grp", None, None)
    return jax.shard_map(
        on_device,
        mesh=mesh,
        in_specs=(wide, wide, wide, wide, wide, P(("sub", "grp"), None), P("sub", "grp", None), P("sub", "grp", None)),
        out_specs=(wide, wide, wide),
        check_vma=False,
    )
```
